128 devices in a mesh: rep: 8 (over x, core), shard: 16 (over z, y).
Axes of the slice: x: 4, y: 4, z: 4, core: 2. Of those that a mesh axis runs over, the one named last changes fastest.
Arguments:
- tokens: bfloat16 [16384, 768], P(('rep', 'shard')), may hold values from -6 to 6
- segments: int32 [16384], P(('rep', 'shard')), may hold values from 0 to 23, as said below
- w_qkv: bfloat16 [768, 2304], P('shard'), may hold values from -0.21875 to 0.21875
- w_out: bfloat16 [768, 768], P('shard'), may hold values from -0.875 to 0.875
- w_up: bfloat16 [768, 3072], P('shard'), may hold values from -0.21875 to 0.21875
- w_down: bfloat16 [3072, 768], P('shard'), may hold values from -0.109375 to 0.109375
- b_query: bfloat16 [768], P('shard'), may hold values from -3 to 3
- b_value: bfloat16 [768], P('shard'), may hold values from -3 to 3
- b_out: bfloat16 [768], P('shard'), may hold values from -3 to 3
- b_up: bfloat16 [3072], P('shard'), may hold values from -3 to 3
- b_down: bfloat16 [768], P('shard'), may hold values from -3 to 3
- ln1_gain: bfloat16 [768], P('shard'), may hold values from 0.5 to 1.5
- ln1_shift: bfloat16 [768], P('shard'), may hold values from -2 to 2
- ln2_gain: bfloat16 [768], P('shard'), may hold values from 0.5 to 1.5
- ln2_shift: bfloat16 [768], P('shard'), may hold values from -2 to 2
- cotangent: bfloat16 [16384, 768], P(('rep', 'shard')), may hold values from -6 to 6
Outputs:
- out_tokens: bfloat16 [16384, 768], P(('rep', 'shard'))
- d_tokens: bfloat16 [16384, 768], P(('rep', 'shard'))
- d_w_qkv: float32 [768, 2304], P('shard')
- d_w_out: float32 [768, 768], P('shard')
- d_w_up: float32 [768, 3072], P('shard')
- d_w_down: float32 [3072, 768], P('shard')
- d_b_query: float32 [768], P('shard')
- d_b_value: float32 [768], P('shard')
- d_b_out: float32 [768], P('shard')
- d_b_up: float32 [3072], P('shard')
- d_b_down: float32 [768], P('shard')
- d_ln1_gain: float32 [768], P('shard')
- d_ln1_shift: float32 [768], P('shard')
- d_ln2_gain: float32 [768], P('shard')
- d_ln2_shift: float32 [768], P('shard')
The draws below stay inside these ranges and needn't reach their ends.
Inputs may be any that keep to these rules, and one draw needn't show every extreme that they name: `segments`: numbers never fall along the tokens. The 2048 tokens of replica group r carry the numbers 3 r, 3 r + 1 and 3 r + 2; the middle document starts on a token of the group's first 128 and ends on one of its last 128, and the other two are shorter than 128 tokens.
All inputs are finite; a program needn't handle non-finite values.
Results may differ from the reference program's by a relative error of at most 0.024.
Values may be sent and summed in bfloat16 or wider, within the bound.
No kernel may reach another device: no remote copies, remote signals or barrier semaphores. Data moves between devices by JAX's collectives and lax.ppermute only.
A program may use at most 128 MiB of HBM per device.

```python
import jax
import jax.numpy as jnp
from jax import lax

D = 768
HD = 64
FF = 3072
TOK_DEV = 128
GROUP = 2048
TOKENS = 16384
N_REP = 8


def draw_segments(key, part):
    key = jax.random.fold_in(key, 11)
    first_key, last_key = jax.random.split(key)
    starts = jax.random.randint(first_key, (N_REP,), 1, TOK_DEV)
    finish = jax.random.randint(last_key, (N_REP,), GROUP - TOK_DEV + 1, GROUP)
    places = jnp.arange(GROUP, dtype=jnp.int32)
    inside = (places[None, :] >= starts[:, None]).astype(jnp.int32) + (places[None, :] >= finish[:, None]).astype(jnp.int32)
    offsets = 3 * jnp.arange(N_REP, dtype=jnp.int32)
    return (offsets[:, None] + inside).reshape(-1).astype(jnp.int32)


def block_scale(own_key, shape, cuts, least, high):
    level, own = 1.0, jax.random.fold_in(own_key, 6)
    for position, blocks in cuts:
        heights = jnp.exp(jax.random.uniform(jax.random.fold_in(own, position), (blocks,), jnp.float32, least / len(cuts), high / len(cuts)))
        level = level * jnp.repeat(heights, shape[position] // blocks).reshape([-1 if axis == position else 1 for axis in range(len(shape))])
    return level


def bell_draw(key, dims, scale, limit, cuts=(), kind=jnp.bfloat16):
    values = jax.random.normal(key, dims, jnp.float32) * scale
    if len(cuts) > 0:
        values = block_scale(key, dims, cuts, -0.22, 0.18) * values
    return jnp.clip(values, min=-limit, max=limit).astype(kind)


def setup_inputs(seed: int = 0) -> dict:
    keys = jax.random.split(jax.random.key(seed), 17)
    return {
        "tokens": bell_draw(keys[0], (TOKENS, D), 1.0, 6.0, ((0, 128),)),
        "segments": draw_segments(jax.random.fold_in(keys[16], 71), 0),
        "w_qkv": bell_draw(keys[2], (D, 3 * D), D ** -0.5, 0.21875, ((0, 16),)),
        "w_out": bell_draw(keys[3], (D, D), (D // 16) ** -0.5, 0.875, ((0, 16),)),
        "w_up": bell_draw(keys[4], (D, FF), D ** -0.5, 0.21875, ((0, 16),)),
        "w_down": bell_draw(keys[5], (FF, D), FF ** -0.5, 0.109375, ((0, 16),)),
        "b_query": bell_draw(keys[6], (D,), 0.5, 3.0, ((0, 16),)),
        "b_value": bell_draw(keys[7], (D,), 0.5, 3.0, ((0, 16),)),
        "b_out": bell_draw(keys[8], (D,), 0.5, 3.0, ((0, 16),)),
        "b_up": bell_draw(keys[9], (FF,), 0.5, 3.0, ((0, 16),)),
        "b_down": bell_draw(keys[10], (D,), 0.5, 3.0, ((0, 16),)),
        "ln1_gain": jnp.clip(1.0 + 0.1 * jax.random.normal(keys[11], (D,), jnp.float32), 0.5, 1.5).astype(jnp.bfloat16),
        "ln1_shift": bell_draw(keys[12], (D,), 0.3, 2.0, ((0, 16),)),
        "ln2_gain": jnp.clip(1.0 + 0.1 * jax.random.normal(keys[13], (D,), jnp.float32), 0.5, 1.5).astype(jnp.bfloat16),
        "ln2_shift": bell_draw(keys[14], (D,), 0.3, 2.0, ((0, 16),)),
        "cotangent": bell_draw(keys[15], (TOKENS, D), 1.0, 6.0, ((0, 128),)),
    }


@jax.custom_vjp
def low(v):
    return lax.optimization_barrier(v.astype(jnp.bfloat16)).astype(jnp.float32)

@jax.custom_vjp
def low_back(v):
    return v

def low_keep(v):
    return (low(v), None)

def low_pass(kept, grad):
    return (grad,)

def back_keep(v):
    return (v, None)

def back_low(kept, grad):
    return (low(grad),)
low.defvjp(low_keep, low_pass)
low_back.defvjp(back_keep, back_low)

def layer_norm(values, gain_vec, shift_vec):
    average = lax.optimization_barrier(jnp.mean(values, axis=-1, keepdims=True))
    centered = values - average
    variance = lax.optimization_barrier(jnp.mean(centered * centered, axis=-1, keepdims=True))
    return centered * lax.rsqrt(variance + 1e-05) * gain_vec + shift_vec

def product(left, right):
    return jnp.dot(left, right, precision=lax.Precision.HIGHEST)

def attend(queries, keys_all, values_all, segments):
    head_count = D // HD
    score_scale = HD ** (-0.5)
    block_rows = min(512, GROUP)
    grouped_q = queries.reshape(N_REP, GROUP, head_count, HD)
    grouped_k = keys_all.reshape(N_REP, GROUP, head_count, HD)
    grouped_v = values_all.reshape(N_REP, GROUP, head_count, HD)
    grouped_s = segments.reshape(N_REP, GROUP)

    def one_group(state_now, items):
        group_q, group_k, group_v, group_s = items
        places = jnp.arange(GROUP, dtype=jnp.int32)

        @jax.checkpoint
        def one_block(block_index):
            first_row = block_index * block_rows
            block_q = lax.dynamic_slice_in_dim(group_q, first_row, block_rows, 0)
            block_seg = lax.dynamic_slice_in_dim(group_s, first_row, block_rows, 0)
            block_pos = first_row + jnp.arange(block_rows, dtype=jnp.int32)
            scores = jnp.einsum('qhd,khd->hqk', block_q, group_k, precision=lax.Precision.HIGHEST) * score_scale
            scores = low_back(scores)
            allowed = (places[None, :] <= block_pos[:, None]) & (group_s[None, :] == block_seg[:, None])
            scores = jnp.where(allowed[None], scores, -1e+30)
            softened = low(jax.nn.softmax(scores, axis=-1))
            return jnp.einsum('hqk,khd->qhd', softened, group_v, precision=lax.Precision.HIGHEST)
        results = lax.map(one_block, jnp.arange(GROUP // block_rows, dtype=jnp.int32))
        return (state_now, results.reshape(GROUP, head_count * HD))
    _, attended = lax.scan(one_group, jnp.zeros((), jnp.float32), (grouped_q, grouped_k, grouped_v, grouped_s))
    return attended.reshape(N_REP * GROUP, head_count * HD)

def reference(tokens, segments, w_qkv, w_out, w_up, w_down, b_query, b_value, b_out, b_up, b_down, ln1_gain, ln1_shift, ln2_gain, ln2_shift, cotangent):
    floats = tuple((item.astype(jnp.float32) for item in (tokens, w_qkv, w_out, w_up, w_down, b_query, b_value, b_out, b_up, b_down, ln1_gain, ln1_shift, ln2_gain, ln2_shift)))

    def forward(inputs, qkv_w, out_w, up_w, down_w, query_b, value_b, out_b, up_b, down_b, gain_one, shift_one, gain_two, shift_two):
        model_width = inputs.shape[1]
        normed = low(layer_norm(inputs, gain_one, shift_one))
        bias_cat = jnp.concatenate([query_b, jnp.zeros_like(query_b), value_b])
        projected = low(low_back(product(normed, qkv_w) + bias_cat))
        attended = attend(projected[:, :model_width], projected[:, model_width:2 * model_width], projected[:, 2 * model_width:], segments)
        attended = low(low_back(attended))
        middle = inputs + low_back(product(attended, out_w) + out_b)
        normed_two = low(layer_norm(middle, gain_two, shift_two))
        upward = low_back(product(normed_two, up_w) + up_b)
        activated = low(jax.nn.gelu(upward))
        return middle + low_back(product(activated, down_w) + down_b)
    result, pull = jax.vjp(forward, *floats)
    grads = pull(cotangent.astype(jnp.float32))
    return (result.astype(jnp.bfloat16), grads[0].astype(jnp.bfloat16), grads[1], grads[2], grads[3], grads[4], grads[5], grads[6], grads[7], grads[8], grads[9], grads[10], grads[11], grads[12], grads[13])
```

```python
import jax
import jax.numpy as jnp
from jax import lax
from jax.experimental import pallas as pl
from jax.experimental.pallas import tpu as pltpu
from jax.sharding import Mesh, PartitionSpec as P

HD = 64
TOK = 128
D = 768
HEADS = 3
WIDTH = HEADS * HD
CHUNK = 512
LOW = jnp.bfloat16
WIDE = jnp.float32


def dot(left, right, dims=((1,), (0,))):
    return lax.dot_general(left, right, (dims, ((), ())), preferred_element_type=WIDE)


def masked(scores, start, place, chunk, block):
    if chunk != block and chunk != 0 and block != 3:
        return scores
    spots = lax.broadcasted_iota(jnp.int32, scores.shape, 0) + chunk * CHUNK
    allowed = None
    if chunk == 0 or block == 3:
        allowed = spots >= start
    if chunk == block:
        causal = spots <= place
        allowed = causal if allowed is None else allowed & causal
    return jnp.where(allowed, scores, -1e30)


def chunk_rows(kv_ref, chunk, low, high):
    return jnp.concatenate(
        [kv_ref[y, chunk * TOK : (chunk + 1) * TOK, low:high] for y in range(4)], axis=0
    )


def forward_kernel(q_ref, kv_ref, bound_ref, att_ref, lse_ref):
    for block in range(4):
        rows = slice(block * TOK, (block + 1) * TOK)
        start = bound_ref[0:1, rows]
        place = bound_ref[1:2, rows]
        for head in range(HEADS):
            cols = slice(head * HD, (head + 1) * HD)
            query = q_ref[rows, cols]
            scores = []
            for chunk in range(block + 1):
                keys = chunk_rows(kv_ref, chunk, head * HD, head * HD + HD)
                scores.append(
                    masked(dot(keys, query, ((1,), (1,))), start, place, chunk, block)
                )
            top = scores[0].max(axis=0, keepdims=True)
            for item in scores[1:]:
                top = jnp.maximum(top, item.max(axis=0, keepdims=True))
            total = jnp.zeros((1, TOK), WIDE)
            summed = jnp.zeros((HD, TOK), WIDE)
            for chunk in range(block + 1):
                weights = jnp.exp(scores[chunk] - top)
                total = total + weights.sum(axis=0, keepdims=True)
                values = chunk_rows(kv_ref, chunk, WIDTH + head * HD, WIDTH + head * HD + HD)
                summed = summed + dot(values, weights.astype(LOW), ((0,), (0,)))
            att_ref[rows, cols] = jnp.transpose(summed / total).astype(LOW)
            lse_ref[head : head + 1, rows] = top + jnp.log(total)


def backward_kernel(q_ref, kv_ref, bound_ref, lse_ref, do_ref, dq_ref, dkv_ref, p_ref, ds_ref):
    for head in range(HEADS):
        cols = slice(head * HD, (head + 1) * HD)
        for block in range(4):
            rows = slice(block * TOK, (block + 1) * TOK)
            start = bound_ref[0:1, rows]
            place = bound_ref[1:2, rows]
            query = q_ref[rows, cols]
            d_out = do_ref[rows, cols]
            lse = lse_ref[head : head + 1, rows]
            delta = jnp.zeros((1, TOK), WIDE)
            probs, d_probs = [], []
            for chunk in range(block + 1):
                keys = chunk_rows(kv_ref, chunk, head * HD, head * HD + HD)
                scores = masked(dot(keys, query, ((1,), (1,))), start, place, chunk, block)
                prob = jnp.exp(scores - lse)
                values = chunk_rows(kv_ref, chunk, WIDTH + head * HD, WIDTH + head * HD + HD)
                d_prob = dot(values, d_out, ((1,), (1,)))
                delta = delta + (prob * d_prob).sum(axis=0, keepdims=True)
                p_ref[chunk * CHUNK : (chunk + 1) * CHUNK, rows] = prob.astype(LOW)
                probs.append(prob)
                d_probs.append(d_prob)
            d_query = jnp.zeros((HD, TOK), WIDE)
            for chunk in range(block + 1):
                d_score = (probs[chunk] * (d_probs[chunk] - delta)).astype(LOW)
                ds_ref[chunk * CHUNK : (chunk + 1) * CHUNK, rows] = d_score
                keys = chunk_rows(kv_ref, chunk, head * HD, head * HD + HD)
                d_query = d_query + dot(keys, d_score, ((0,), (0,)))
            dq_ref[rows, cols] = (jnp.transpose(d_query) * (HD**-0.5)).astype(LOW)
        for chunk in range(4):
            spots = slice(chunk * CHUNK, (chunk + 1) * CHUNK)
            later = slice(chunk * TOK, 4 * TOK)
            d_keys = dot(ds_ref[spots, later], q_ref[later, cols]).astype(LOW)
            d_values = dot(p_ref[spots, later], do_ref[later, cols]).astype(LOW)
            for y in range(4):
                part = slice(y * TOK, (y + 1) * TOK)
                place_rows = slice(chunk * TOK, (chunk + 1) * TOK)
                dkv_ref[y, place_rows, cols] = d_keys[part]
                dkv_ref[y, place_rows, WIDTH + head * HD : WIDTH + head * HD + HD] = d_values[part]


VMEM = pl.BlockSpec(memory_space=pltpu.VMEM)
PARAMS = pltpu.CompilerParams(vmem_limit_bytes=48 * 1024 * 1024)


def attend_forward(query, kv, bounds):
    return pl.pallas_call(
        forward_kernel,
        out_shape=(
            jax.ShapeDtypeStruct((4 * TOK, WIDTH), LOW),
            jax.ShapeDtypeStruct((8, 4 * TOK), WIDE),
        ),
        in_specs=[VMEM] * 3,
        out_specs=(VMEM, VMEM),
        compiler_params=PARAMS,
        cost_estimate=pl.CostEstimate(
            flops=1_000_000_000, bytes_accessed=4_000_000, transcendentals=2_000_000
        ),
    )(query, kv, bounds)


def attend_backward(query, kv, bounds, lse, d_out):
    return pl.pallas_call(
        backward_kernel,
        out_shape=(
            jax.ShapeDtypeStruct((4 * TOK, WIDTH), LOW),
            jax.ShapeDtypeStruct((4, 4 * TOK, 2 * WIDTH), LOW),
        ),
        in_specs=[VMEM] * 5,
        out_specs=(VMEM, VMEM),
        scratch_shapes=[
            pltpu.VMEM((4 * CHUNK, 4 * TOK), LOW),
            pltpu.VMEM((4 * CHUNK, 4 * TOK), LOW),
        ],
        compiler_params=PARAMS,
        cost_estimate=pl.CostEstimate(
            flops=2_500_000_000, bytes_accessed=6_000_000, transcendentals=2_000_000
        ),
    )(query, kv, bounds, lse, d_out)


def norm_parts(values):
    average = jnp.mean(values, axis=-1, keepdims=True)
    centered = values - average
    variance = jnp.mean(centered * centered, axis=-1, keepdims=True)
    inverse = lax.rsqrt(variance + 1e-05)
    return centered * inverse, inverse


def norm_back(hat, inverse, gain, grad):
    scaled = grad * gain
    mean_one = jnp.mean(scaled, axis=-1, keepdims=True)
    mean_two = jnp.mean(scaled * hat, axis=-1, keepdims=True)
    d_values = inverse * (scaled - mean_one - hat * mean_two)
    return d_values, jnp.sum(grad * hat, axis=0), jnp.sum(grad, axis=0)


def swap(value, axis):
    return lax.all_to_all(value, axis, 0, 0, tiled=True)


def sum_swap(value, axis):
    moved = swap(value, axis)
    return jnp.sum(moved.astype(WIDE), axis=0)


def pad_rows(value, count):
    return jnp.pad(value, ((0, count - value.shape[0]), (0, 0)))


def body(
    tokens,
    segments,
    w_qkv,
    w_out,
    w_up,
    w_down,
    b_query,
    b_value,
    b_out,
    b_up,
    b_down,
    ln1_gain,
    ln1_shift,
    ln2_gain,
    ln2_shift,
    cotangent,
):
    ix, ic, iz, iy = (lax.axis_index(name) for name in ("x", "c", "z", "y"))
    first_doc = 3 * (2 * ix + ic)

    counts = jnp.stack(
        [jnp.sum(segments <= first_doc), jnp.sum(segments <= first_doc + 1)]
    ).astype(LOW)
    small = jnp.concatenate(
        [b_query, b_value, b_out, b_down, ln1_gain, ln1_shift, ln2_gain, ln2_shift, b_up]
    )
    small_rows = jnp.stack([small, jnp.pad(counts, (0, small.shape[0] - 2))])
    head_part = w_qkv.reshape(48, 3, 4, WIDTH).transpose(2, 0, 1, 3).reshape(4, 48, 3 * WIDTH)
    early = jnp.concatenate(
        [head_part, jnp.broadcast_to(pad_rows(small_rows, 16)[None], (4, 16, 3 * WIDTH))], axis=1
    )
    early = swap(early, "z")
    early_y = jnp.concatenate(
        [
            early[:, :48].reshape(192, 3 * WIDTH),
            pad_rows(early[:, 48:50].reshape(8, 3 * WIDTH), 16),
        ],
        axis=0,
    )
    early_all = lax.all_gather(early_y, "y")
    qkv_part = early_all[:, :192].reshape(4, 4, 48, 3 * WIDTH).swapaxes(0, 1).reshape(D, 3 * WIDTH)
    small_all = early_all[:, 192:200].reshape(4, 4, 2, 576).swapaxes(0, 1).astype(WIDE)
    vectors = small_all[:, :, 0]
    total_counts = jnp.sum(small_all[:, :, 1, :2], axis=(0, 1)).astype(jnp.int32)
    wide = vectors[:, :, : 8 * 48].reshape(16, 8, 48).swapaxes(0, 1).reshape(8, D)
    bias_out, bias_down, gain_one, shift_one, gain_two, shift_two = (
        wide[index] for index in range(2, 8)
    )
    own = lax.dynamic_index_in_dim(vectors, iz, 0, keepdims=False)
    bias_query = own[:, :48].reshape(WIDTH)
    bias_value = own[:, 48:96].reshape(WIDTH)
    bias_up = own[:, 384:].reshape(D)

    late = jnp.concatenate(
        [
            w_up.reshape(48, 4, D).swapaxes(0, 1),
            jnp.broadcast_to(w_out[None], (4, 48, D)),
        ],
        axis=1,
    )
    late = swap(late, "z")
    late_y = jnp.concatenate(
        [late[:, :48].reshape(192, D), late[:, 48:].reshape(192, D), w_down], axis=0
    )
    late_all = lax.all_gather(late_y, "y")
    up_part = late_all[:, :192].reshape(4, 4, 48, D).swapaxes(0, 1).reshape(D, D)
    out_full = late_all[:, 192:384].reshape(4, 4, 48, D).swapaxes(0, 1).reshape(D, D)
    down_part = late_all[:, 384:].reshape(D, D)

    seg_row = jnp.pad(segments.astype(LOW)[None], ((0, 15), (0, D - TOK)))
    token_all = lax.all_gather(jnp.concatenate([tokens, seg_row], axis=0), "z")
    inputs = token_all[:, :TOK].reshape(4 * TOK, D).astype(WIDE)
    seg_all = token_all[:, TOK, :TOK].astype(jnp.int32)
    cot_all = lax.all_gather(cotangent, "z", tiled=True)
    start = jnp.where(
        seg_all <= first_doc, 0, jnp.where(seg_all <= first_doc + 1, total_counts[0], total_counts[1])
    )
    place = (
        4 * TOK * jnp.arange(4, dtype=jnp.int32)[:, None]
        + TOK * iy
        + jnp.arange(TOK, dtype=jnp.int32)[None, :]
    )
    bounds = jnp.concatenate(
        [start.reshape(1, 4 * TOK), place.reshape(1, 4 * TOK), jnp.zeros((6, 4 * TOK), jnp.int32)]
    )

    hat_one, inverse_one = norm_parts(inputs)
    normed_one = (hat_one * gain_one + shift_one).astype(LOW)
    qkv = dot(normed_one, qkv_part)
    query = ((qkv[:, :WIDTH] + bias_query).astype(LOW) * (HD**-0.5)).astype(LOW)
    kv = jnp.concatenate(
        [qkv[:, WIDTH : 2 * WIDTH], qkv[:, 2 * WIDTH :] + bias_value], axis=1
    ).astype(LOW)
    kv_all = lax.all_gather(kv, "y")
    att_part, lse = attend_forward(query, kv_all, bounds)
    att_all = lax.all_gather(att_part, "z")
    attended = jnp.concatenate([att_all[index] for index in range(4)], axis=1)

    middle = inputs + dot(attended, out_full) + bias_out
    hat_two, inverse_two = norm_parts(middle)
    normed_two = (hat_two * gain_two + shift_two).astype(LOW)
    upward = dot(normed_two, up_part) + bias_up
    activated, pull = jax.vjp(jax.nn.gelu, upward)
    activated = activated.astype(LOW)
    (d_upward,) = pull(dot(cot_all, down_part, ((1,), (1,))))
    d_upward = d_upward.astype(LOW)
    pair = jnp.concatenate(
        [
            dot(activated, down_part).astype(LOW).reshape(4, TOK, D),
            dot(d_upward, up_part, ((1,), (1,))).astype(LOW).reshape(4, TOK, D),
        ],
        axis=2,
    )
    pair = sum_swap(pair, "z")
    own_rows = iz * TOK
    middle_own = lax.dynamic_slice_in_dim(middle, own_rows, TOK, 0)
    out_tokens = (middle_own + pair[:, :D] + bias_down).astype(LOW)
    hat_own = lax.dynamic_slice_in_dim(hat_two, own_rows, TOK, 0)
    inverse_own = lax.dynamic_slice_in_dim(inverse_two, own_rows, TOK, 0)
    d_norm, d_gain_two, d_shift_two = norm_back(hat_own, inverse_own, gain_two, pair[:, D:])
    d_middle = cotangent.astype(WIDE) + d_norm
    d_branch = lax.all_gather(d_middle.astype(LOW), "z", tiled=True)
    out_rows = lax.dynamic_slice_in_dim(out_full, iz * WIDTH, WIDTH, 0)
    d_attended = dot(d_branch, out_rows, ((1,), (1,))).astype(LOW)

    d_up = dot(normed_two, d_upward, ((0,), (0,))).astype(LOW)
    d_down = dot(activated, cot_all, ((0,), (0,))).astype(LOW)
    d_out = dot(att_part, d_branch, ((0,), (0,))).astype(LOW)
    first_grads = jnp.concatenate(
        [
            d_up.reshape(4, 4, 48, D).swapaxes(0, 1).reshape(4, 192, D),
            d_down.reshape(4, 192, D),
            d_out.reshape(4, 48, D),
        ],
        axis=1,
    )
    first_sum = lax.psum_scatter(first_grads, "y", scatter_dimension=0, tiled=False)

    d_query, d_kv = attend_backward(query, kv_all, bounds, lse, d_attended)
    d_kv = sum_swap(d_kv, "y").astype(LOW)
    d_qkv = jnp.concatenate([d_query, d_kv], axis=1)
    d_normed = dot(d_qkv, qkv_part, ((1,), (1,))).astype(LOW).reshape(4, TOK, D)
    d_normed = sum_swap(d_normed, "z")
    hat_own = lax.dynamic_slice_in_dim(hat_one, own_rows, TOK, 0)
    inverse_own = lax.dynamic_slice_in_dim(inverse_one, own_rows, TOK, 0)
    d_norm, d_gain_one, d_shift_one = norm_back(hat_own, inverse_own, gain_one, d_normed)
    d_tokens = (d_middle + d_norm).astype(LOW)
    d_qkv_w = dot(normed_one, d_qkv, ((0,), (0,))).astype(LOW)

    def own_part(vector):
        return lax.dynamic_index_in_dim(vector.reshape(4, 4, 48), iz, 0, keepdims=False)

    d_qkv_sum = jnp.sum(d_qkv.astype(WIDE), axis=0)
    d_bias_out = own_part(jnp.sum(d_branch.astype(WIDE), axis=0))
    d_bias_down = own_part(jnp.sum(cot_all.astype(WIDE), axis=0))
    d_bias_up = jnp.sum(d_upward.astype(WIDE), axis=0).reshape(4, 192)
    norms = jnp.stack([d_gain_one, d_shift_one, d_gain_two, d_shift_two])
    norms = norms.reshape(4, 4, 4, 48).transpose(2, 1, 0, 3).reshape(4, D)
    smalls = jnp.concatenate(
        [
            norms,
            d_qkv_sum[:WIDTH].reshape(4, 48),
            d_qkv_sum[2 * WIDTH :].reshape(4, 48),
            d_bias_out,
            d_bias_down,
            d_bias_up,
        ],
        axis=1,
    ).astype(LOW)
    second_grads = jnp.concatenate(
        [
            d_qkv_w.reshape(4, 4, 48, 3 * WIDTH).swapaxes(0, 1).reshape(4, 192, 3 * WIDTH),
            jnp.pad(smalls.reshape(4, 2, 576), ((0, 0), (0, 14), (0, 0))),
        ],
        axis=1,
    )
    second_sum = sum_swap(second_grads, "y").astype(LOW)

    small_sum = second_sum[192:194].reshape(2 * 576)
    norm_rows = jnp.pad(small_sum[:D].reshape(4, 1, 192), ((0, 0), (0, 15), (0, 3 * WIDTH - 192)))
    moved_qkv = swap(
        jnp.concatenate([second_sum[:192].reshape(4, 48, 3 * WIDTH), norm_rows], axis=1), "z"
    )
    moved_up = swap(first_sum[:192].reshape(4, 48, D), "z")
    norm_sum = jnp.sum(moved_qkv[:, 48, :192].astype(WIDE), axis=0).astype(LOW)
    qkv_rows = (
        moved_qkv[:, :48].reshape(4, 48, 3, WIDTH).transpose(2, 1, 0, 3).reshape(3 * 48, D)
    )
    small_row = jnp.concatenate([norm_sum, small_sum[D:], jnp.zeros((192,), LOW)])
    packed = jnp.concatenate(
        [
            qkv_rows,
            moved_up.reshape(192, D),
            first_sum[192:],
            pad_rows(small_row[None], 64),
        ],
        axis=0,
    )

    halves = packed.reshape(2, 320, D)
    mine = lax.dynamic_index_in_dim(halves, ic, 0, keepdims=False)
    theirs = lax.dynamic_index_in_dim(halves, 1 - ic, 0, keepdims=False)
    got = lax.ppermute(theirs, "c", [(0, 1), (1, 0)])
    half = (mine.astype(WIDE) + got.astype(WIDE)).astype(LOW)
    piece = sum_swap(half.reshape(4, 80, D), "x").astype(LOW)
    half = lax.all_gather(piece, "x", tiled=True)
    whole = lax.all_gather(half, "c", tiled=True).astype(WIDE)

    d_w_qkv = jnp.concatenate([whole[48 * i : 48 * i + 48] for i in range(3)], axis=1)
    d_w_up = jnp.concatenate([whole[144 + 48 * i : 192 + 48 * i] for i in range(4)], axis=1)
    d_w_down = whole[336:528]
    d_w_out = whole[528:576]
    line = whole[576]
    return (
        out_tokens,
        d_tokens,
        d_w_qkv,
        d_w_out,
        d_w_up,
        d_w_down,
        line[192:240],
        line[240:288],
        line[288:336],
        line[384:576],
        line[336:384],
        line[0:48],
        line[48:96],
        line[96:144],
        line[144:192],
    )


def solution(mesh):
    parts = Mesh(mesh.devices.reshape(4, 2, 4, 4), ("x", "c", "z", "y"))
    every = ("x", "c", "z", "y")
    group = ("z", "y")
    row, line = P(group, None), P(group)
    return jax.shard_map(
        body,
        mesh=parts,
        in_specs=(P(every, None), P(every)) + (row,) * 4 + (line,) * 9 + (P(every, None),),
        out_specs=(P(every, None),) * 2 + (row,) * 4 + (line,) * 9,
        check_vma=False,
    )
```

```python
import jax
import jax.numpy as jnp
from jax import lax
from jax.experimental import pallas as pl
from jax.experimental.pallas import tpu as pltpu
from jax.sharding import Mesh, PartitionSpec as P

HD = 64
TOK = 128
D = 768
HEADS = 3
WIDTH = HEADS * HD
CHUNK = 512
LOW = jnp.bfloat16
WIDE = jnp.float32


def dot(left, right, dims=((1,), (0,))):
    return lax.dot_general(left, right, (dims, ((), ())), preferred_element_type=WIDE)


def masked(scores, start, place, chunk, block):
    if chunk != block and chunk != 0 and block != 3:
        return scores
    spots = lax.broadcasted_iota(jnp.int32, scores.shape, 0) + chunk * CHUNK
    allowed = None
    if chunk == 0 or block == 3:
        allowed = spots >= start
    if chunk == block:
        causal = spots <= place
        allowed = causal if allowed is None else allowed & causal
    return jnp.where(allowed, scores, -1e30)


def chunk_rows(kv_ref, chunk, low, high):
    return jnp.concatenate(
        [kv_ref[y, chunk * TOK : (chunk + 1) * TOK, low:high] for y in range(4)], axis=0
    )


def forward_kernel(q_ref, kv_ref, bound_ref, att_ref, lse_ref):
    for block in range(4):
        rows = slice(block * TOK, (block + 1) * TOK)
        start = bound_ref[0:1, rows]
        place = bound_ref[1:2, rows]
        for head in range(HEADS):
            cols = slice(head * HD, (head + 1) * HD)
            query = q_ref[rows, cols]
            scores = []
            for chunk in range(block + 1):
                keys = chunk_rows(kv_ref, chunk, head * HD, head * HD + HD)
                scores.append(
                    masked(dot(keys, query, ((1,), (1,))), start, place, chunk, block)
                )
            top = scores[0].max(axis=0, keepdims=True)
            for item in scores[1:]:
                top = jnp.maximum(top, item.max(axis=0, keepdims=True))
            total = jnp.zeros((1, TOK), WIDE)
            summed = jnp.zeros((HD, TOK), WIDE)
            for chunk in range(block + 1):
                weights = jnp.exp(scores[chunk] - top)
                total = total + weights.sum(axis=0, keepdims=True)
                values = chunk_rows(kv_ref, chunk, WIDTH + head * HD, WIDTH + head * HD + HD)
                summed = summed + dot(values, weights.astype(LOW), ((0,), (0,)))
            att_ref[rows, cols] = jnp.transpose(summed / total).astype(LOW)
            lse_ref[head : head + 1, rows] = top + jnp.log(total)


def backward_kernel(q_ref, kv_ref, bound_ref, lse_ref, do_ref, dq_ref, dkv_ref, p_ref, ds_ref):
    for head in range(HEADS):
        cols = slice(head * HD, (head + 1) * HD)
        for block in range(4):
            rows = slice(block * TOK, (block + 1) * TOK)
            start = bound_ref[0:1, rows]
            place = bound_ref[1:2, rows]
            query = q_ref[rows, cols]
            d_out = do_ref[rows, cols]
            lse = lse_ref[head : head + 1, rows]
            delta = jnp.zeros((1, TOK), WIDE)
            probs, d_probs = [], []
            for chunk in range(block + 1):
                keys = chunk_rows(kv_ref, chunk, head * HD, head * HD + HD)
                scores = masked(dot(keys, query, ((1,), (1,))), start, place, chunk, block)
                prob = jnp.exp(scores - lse)
                values = chunk_rows(kv_ref, chunk, WIDTH + head * HD, WIDTH + head * HD + HD)
                d_prob = dot(values, d_out, ((1,), (1,)))
                delta = delta + (prob * d_prob).sum(axis=0, keepdims=True)
                p_ref[chunk * CHUNK : (chunk + 1) * CHUNK, rows] = prob.astype(LOW)
                probs.append(prob)
                d_probs.append(d_prob)
            d_query = jnp.zeros((HD, TOK), WIDE)
            for chunk in range(block + 1):
                d_score = (probs[chunk] * (d_probs[chunk] - delta)).astype(LOW)
                ds_ref[chunk * CHUNK : (chunk + 1) * CHUNK, rows] = d_score
                keys = chunk_rows(kv_ref, chunk, head * HD, head * HD + HD)
                d_query = d_query + dot(keys, d_score, ((0,), (0,)))
            dq_ref[rows, cols] = (jnp.transpose(d_query) * (HD**-0.5)).astype(LOW)
        for chunk in range(4):
            spots = slice(chunk * CHUNK, (chunk + 1) * CHUNK)
            later = slice(chunk * TOK, 4 * TOK)
            d_keys = dot(ds_ref[spots, later], q_ref[later, cols]).astype(LOW)
            d_values = dot(p_ref[spots, later], do_ref[later, cols]).astype(LOW)
            for y in range(4):
                part = slice(y * TOK, (y + 1) * TOK)
                place_rows = slice(chunk * TOK, (chunk + 1) * TOK)
                dkv_ref[y, place_rows, cols] = d_keys[part]
                dkv_ref[y, place_rows, WIDTH + head * HD : WIDTH + head * HD + HD] = d_values[part]


def pack_kernel(tokens_ref, qkv_ref, up_ref, short_ref, hidden_ref, seg_ref, out_ref):
    seg = seg_ref[...]
    count_one = jnp.sum((seg <= 0).astype(WIDE), axis=1, keepdims=True)
    count_two = jnp.sum((seg <= 1).astype(WIDE), axis=1, keepdims=True)
    spot = lax.broadcasted_iota(jnp.int32, (1, 192), 1)
    counts = jnp.where(spot == 0, count_one, jnp.where(spot == 1, count_two, 0.0))
    side = jnp.concatenate(
        [
            jnp.concatenate(
                [short_ref[...].astype(WIDE), jnp.zeros((8, 144), WIDE)], axis=1
            ),
            jnp.concatenate(
                [hidden_ref[...].astype(WIDE), jnp.zeros((4, 144), WIDE)], axis=1
            ),
            counts,
            jnp.concatenate([seg.astype(WIDE), jnp.zeros((1, 64), WIDE)], axis=1),
            jnp.zeros((34, 192), WIDE),
        ],
        axis=0,
    ).astype(LOW)
    for part in range(4):
        out_ref[part, 0:TOK, :] = tokens_ref[...]
        for kind in range(3):
            out_ref[part, TOK : TOK + 48, kind * WIDTH : (kind + 1) * WIDTH] = qkv_ref[
                :, kind * D + part * WIDTH : kind * D + (part + 1) * WIDTH
            ]
        out_ref[part, TOK : TOK + 48, 3 * WIDTH : D] = side
        out_ref[part, TOK + 48 : TOK + 96, :] = up_ref[:, part * D : (part + 1) * D]


def unpack_kernel(core_ref, mine_ref, theirs_ref, qkv_ref, out_ref, up_ref, down_ref, *line_refs):
    first = core_ref[0] == 0
    half = D // 2
    short = jnp.zeros((12, 48), WIDE)
    for part in range(4):
        mine = mine_ref[part].astype(WIDE)
        theirs = theirs_ref[part].astype(WIDE)
        sides = (jnp.where(first, mine, theirs), jnp.where(first, theirs, mine))
        rows = slice(24 * (part % 2), 24 * (part % 2) + 24)
        for core in range(2):
            side = sides[core]
            cols = slice(core * half, (core + 1) * half)
            if part < 3:
                down_ref[part * 64 : (part + 1) * 64, cols] = side[96:160]
            else:
                out_ref[:, cols] = side[96:144]
            for quarter in range(4):
                block = side[24 * quarter : 24 * quarter + 24]
                if part < 2:
                    low = quarter * D + core * half
                    up_ref[rows, low : low + half] = block
                    continue
                low = quarter * WIDTH
                if core == 0:
                    qkv_ref[rows, low : low + WIDTH] = block[:, :WIDTH]
                    qkv_ref[rows, D + low : D + low + WIDTH] = block[:, WIDTH:]
                else:
                    qkv_ref[rows, 2 * D + low : 2 * D + low + WIDTH] = block[:, :WIDTH]
                    if part == 2:
                        short = short + block[:12, WIDTH : WIDTH + 48]
    hidden = jnp.concatenate([short[2 + i : 3 + i] for i in range(4)], axis=1)
    lines = [short[i : i + 1] for i in (0, 1, 6)] + [hidden]
    lines += [short[i : i + 1] for i in range(7, 12)]
    for ref, value in zip(line_refs, lines):
        ref[...] = value


VMEM = pl.BlockSpec(memory_space=pltpu.VMEM)
PARAMS = pltpu.CompilerParams(vmem_limit_bytes=48 * 1024 * 1024)


def attend_forward(query, kv, bounds):
    return pl.pallas_call(
        forward_kernel,
        out_shape=(
            jax.ShapeDtypeStruct((4 * TOK, WIDTH), LOW),
            jax.ShapeDtypeStruct((8, 4 * TOK), WIDE),
        ),
        in_specs=[VMEM] * 3,
        out_specs=(VMEM, VMEM),
        compiler_params=PARAMS,
        cost_estimate=pl.CostEstimate(
            flops=1_000_000_000, bytes_accessed=4_000_000, transcendentals=2_000_000
        ),
    )(query, kv, bounds)


def attend_backward(query, kv, bounds, lse, d_out):
    return pl.pallas_call(
        backward_kernel,
        out_shape=(
            jax.ShapeDtypeStruct((4 * TOK, WIDTH), LOW),
            jax.ShapeDtypeStruct((4, 4 * TOK, 2 * WIDTH), LOW),
        ),
        in_specs=[VMEM] * 5,
        out_specs=(VMEM, VMEM),
        scratch_shapes=[
            pltpu.VMEM((4 * CHUNK, 4 * TOK), LOW),
            pltpu.VMEM((4 * CHUNK, 4 * TOK), LOW),
        ],
        compiler_params=PARAMS,
        cost_estimate=pl.CostEstimate(
            flops=2_500_000_000, bytes_accessed=6_000_000, transcendentals=2_000_000
        ),
    )(query, kv, bounds, lse, d_out)


def pack(tokens, w_qkv, w_up, short, hidden, segments):
    return pl.pallas_call(
        pack_kernel,
        out_shape=jax.ShapeDtypeStruct((4, TOK + 96, D), LOW),
        in_specs=[VMEM] * 6,
        out_specs=VMEM,
        compiler_params=PARAMS,
        cost_estimate=pl.CostEstimate(
            flops=1_000_000, bytes_accessed=2_500_000, transcendentals=0
        ),
    )(tokens, w_qkv, w_up, short, hidden, segments)


def unpack(core, mine, theirs):
    return pl.pallas_call(
        unpack_kernel,
        out_shape=tuple(
            jax.ShapeDtypeStruct(shape, WIDE)
            for shape in ((48, 3 * D), (48, D), (48, 4 * D), (192, D))
            + ((1, 48),) * 3
            + ((1, 192),)
            + ((1, 48),) * 5
        ),
        in_specs=[pl.BlockSpec(memory_space=pltpu.SMEM), VMEM, VMEM],
        out_specs=(VMEM,) * 13,
        compiler_params=PARAMS,
        cost_estimate=pl.CostEstimate(
            flops=1_000_000, bytes_accessed=3_500_000, transcendentals=0
        ),
    )(core, mine, theirs)


def norm_parts(values):
    average = jnp.mean(values, axis=-1, keepdims=True)
    centered = values - average
    variance = jnp.mean(centered * centered, axis=-1, keepdims=True)
    inverse = lax.rsqrt(variance + 1e-05)
    return centered * inverse, inverse


def norm_back(hat, inverse, gain, grad):
    scaled = grad * gain
    mean_one = jnp.mean(scaled, axis=-1, keepdims=True)
    mean_two = jnp.mean(scaled * hat, axis=-1, keepdims=True)
    return inverse * (scaled - mean_one - hat * mean_two)


def swap(value, axis):
    return lax.all_to_all(value, axis, 0, 0, tiled=True)


def share(value, axis):
    return swap(jnp.broadcast_to(value[None], (4,) + value.shape), axis)


def total(value):
    return jnp.sum(value.astype(WIDE), axis=0)


def other_core(value):
    return lax.ppermute(value, "c", [(0, 1), (1, 0)])


def body(
    tokens,
    segments,
    w_qkv,
    w_out,
    w_up,
    w_down,
    b_query,
    b_value,
    b_out,
    b_up,
    b_down,
    ln1_gain,
    ln1_shift,
    ln2_gain,
    ln2_shift,
    cotangent,
):
    ix, ic, iz, iy = (lax.axis_index(name) for name in ("x", "c", "z", "y"))
    first_doc = 3 * (2 * ix + ic)
    half = D // 2

    def lanes(value, core):
        return lax.dynamic_slice_in_dim(value, core * half, half, value.ndim - 1)

    short = jnp.stack(
        [b_query, b_value, b_out, b_down, ln1_gain, ln1_shift, ln2_gain, ln2_shift]
    )
    early = pack(
        tokens, w_qkv, w_up, short, b_up.reshape(4, 48), (segments - first_doc)[None]
    )
    early = swap(early, "z")
    token_all = early[:, :TOK].reshape(4 * TOK, D)
    seg_all = early[:, TOK + 13, 576:704].astype(jnp.int32)
    early_all = share(early[:, TOK : TOK + 48, :640], "y").swapaxes(0, 1)
    qkv_part = early_all[:, :, :, :576].reshape(D, 3 * WIDTH)
    small_all = early_all[:, :, :16, 576:624].astype(WIDE)
    total_counts = jnp.sum(small_all[:, :, 12, :2], axis=(0, 1)).astype(jnp.int32)
    wide = small_all.reshape(16, 16, 48)[:, :8].swapaxes(0, 1).reshape(8, D)
    bias_out, bias_down, gain_one, shift_one, gain_two, shift_two = (
        wide[index] for index in range(2, 8)
    )
    own = lax.dynamic_index_in_dim(small_all, iz, 0, keepdims=False)
    bias_query = own[:, 0].reshape(WIDTH)
    bias_value = own[:, 1].reshape(WIDTH)
    bias_up = own[:, 8:12].reshape(D)

    plain = lax.all_gather(jnp.concatenate([w_down, w_out], axis=0), "y")
    down_part = plain[:, :192].reshape(D, D)
    gathered = lax.all_gather(
        jnp.concatenate([cotangent, plain[:, 192:].reshape(192, D)], axis=0), "z"
    )
    cot_all = gathered[:, :TOK].reshape(4 * TOK, D)
    out_full = gathered[:, TOK:].reshape(D, D)
    up_part = lax.all_gather(early[:, TOK + 48 :].reshape(192, D), "y")
    up_part = up_part.reshape(4, 4, 48, D).swapaxes(0, 1).reshape(D, D)

    inputs = token_all.astype(WIDE)
    start = jnp.where(
        seg_all <= 0, 0, jnp.where(seg_all <= 1, total_counts[0], total_counts[1])
    )
    place = (
        4 * TOK * jnp.arange(4, dtype=jnp.int32)[:, None]
        + TOK * iy
        + jnp.arange(TOK, dtype=jnp.int32)[None, :]
    )
    bounds = jnp.concatenate(
        [start.reshape(1, 4 * TOK), place.reshape(1, 4 * TOK), jnp.zeros((6, 4 * TOK), jnp.int32)]
    )

    hat_one, inverse_one = norm_parts(inputs)
    normed_one = (hat_one * gain_one + shift_one).astype(LOW)
    qkv = dot(normed_one, qkv_part)
    query = ((qkv[:, :WIDTH] + bias_query).astype(LOW) * (HD**-0.5)).astype(LOW)
    kv = jnp.concatenate(
        [qkv[:, WIDTH : 2 * WIDTH], qkv[:, 2 * WIDTH :] + bias_value], axis=1
    ).astype(LOW)
    kv_all = share(kv, "y")
    att_part, lse = attend_forward(query, kv_all, bounds)
    att_all = share(att_part, "z")
    attended = jnp.concatenate([att_all[index] for index in range(4)], axis=1)

    middle = inputs + dot(attended, out_full) + bias_out
    hat_two, inverse_two = norm_parts(middle)
    normed_two = (hat_two * gain_two + shift_two).astype(LOW)
    upward = dot(normed_two, up_part) + bias_up
    activated, pull = jax.vjp(jax.nn.gelu, upward)
    activated = activated.astype(LOW)
    (d_upward,) = pull(dot(cot_all, down_part, ((1,), (1,))))
    d_upward = d_upward.astype(LOW)
    d_normed = dot(d_upward, up_part, ((1,), (1,)))
    d_gain_two = jnp.sum(d_normed * hat_two, axis=0)
    d_shift_two = jnp.sum(d_normed, axis=0)
    d_normed = total(swap(d_normed.astype(LOW).reshape(4, TOK, D), "z"))
    own_rows = iz * TOK

    def mine(value):
        return lax.dynamic_slice_in_dim(value, own_rows, TOK, 0)

    out_part = dot(activated, down_part).astype(LOW).reshape(4, TOK, D)
    d_middle = cotangent.astype(WIDE) + norm_back(
        mine(hat_two), mine(inverse_two), gain_two, d_normed
    )
    d_branch = d_middle.astype(LOW)
    branch_all = share(d_branch, "z").reshape(4 * TOK, D)
    out_rows = lax.dynamic_slice_in_dim(out_full, iz * WIDTH, WIDTH, 0)
    d_attended = dot(branch_all, out_rows, ((1,), (1,))).astype(LOW)

    def pair_sum(left, right):
        sent = dot(left, lanes(right, 1 - ic), ((0,), (0,))).astype(LOW)
        kept = dot(left, lanes(right, ic), ((0,), (0,)))
        return (kept + other_core(sent).astype(WIDE)).astype(LOW)

    d_up = pair_sum(normed_two, d_upward).reshape(4, 4, 48, half).swapaxes(0, 1)
    first = jnp.concatenate(
        [
            d_up.reshape(4, 192, half),
            pair_sum(activated, cot_all).reshape(4, 192, half),
            pair_sum(att_part, branch_all).reshape(4, 48, half),
        ],
        axis=1,
    )
    first = lax.psum_scatter(first, "y", scatter_dimension=0)
    rows = jnp.pad(first[192:], ((0, 16), (0, 0))).reshape(4, 64, half)
    rows = lax.psum_scatter(rows, "x", scatter_dimension=0)

    d_query, d_kv = attend_backward(query, kv_all, bounds, lse, d_attended)
    d_kv = total(swap(d_kv, "y")).astype(LOW)
    d_qkv = jnp.concatenate([d_query, d_kv], axis=1)
    d_normed = dot(d_qkv, qkv_part, ((1,), (1,)))
    d_gain_one = jnp.sum(d_normed * hat_one, axis=0)
    d_shift_one = jnp.sum(d_normed, axis=0)
    last = jnp.concatenate([d_normed.astype(LOW).reshape(4, TOK, D), out_part], axis=2)
    last = lax.psum_scatter(last, "z", scatter_dimension=0).astype(WIDE)
    d_normed = last[:, :D]
    out_tokens = (mine(middle) + last[:, D:] + bias_down).astype(LOW)
    d_tokens = (
        d_middle + norm_back(mine(hat_one), mine(inverse_one), gain_one, d_normed)
    ).astype(LOW)
    d_qkv_w = dot(normed_one, d_qkv, ((0,), (0,))).astype(LOW)

    d_qkv_sum = jnp.sum(d_qkv.astype(WIDE), axis=0)
    here = (jnp.arange(4) == iz).astype(WIDE)[:, None, None, None]
    of_z = jnp.concatenate(
        [
            d_qkv_sum[:WIDTH].reshape(4, 1, 48),
            d_qkv_sum[2 * WIDTH :].reshape(4, 1, 48),
            jnp.sum(d_upward.astype(WIDE), axis=0).reshape(4, 4, 48),
        ],
        axis=1,
    )
    of_all = jnp.stack(
        [
            jnp.sum(d_branch.astype(WIDE), axis=0),
            jnp.sum(cotangent.astype(WIDE), axis=0),
            d_gain_one,
            d_shift_one,
            d_gain_two,
            d_shift_two,
        ]
    )
    smalls = jnp.concatenate(
        [
            (of_z[None] * here).reshape(16, 6, 48),
            of_all.reshape(6, 16, 48).swapaxes(0, 1),
        ],
        axis=1,
    )
    smalls = jnp.pad(smalls.astype(LOW), ((0, 0), (0, 36), (0, 144)))
    second = jnp.concatenate([d_qkv_w.reshape(16, 48, 576), smalls], axis=2)
    got = other_core(lanes(second, 1 - ic))
    second = (lanes(second, ic).astype(WIDE) + got.astype(WIDE)).astype(LOW)
    second = second.reshape(4, 4, 48, half).swapaxes(0, 1).reshape(4, 192, half)
    second = total(swap(second, "y")).astype(LOW)

    joint = jnp.concatenate(
        [first[:192].reshape(4, 48, half), second.reshape(4, 48, half)], axis=1
    )
    joint = joint.reshape(4, 4, 24, half).swapaxes(0, 1).reshape(16, 24, half)
    joint = total(swap(joint, ("x", "z")).reshape(4, 4, 24, half)).astype(LOW)
    whole = share(jnp.concatenate([joint.reshape(96, half), rows], axis=0), "x")
    theirs = other_core(whole)
    grads = unpack(ic.astype(jnp.int32)[None], whole, theirs)
    return (out_tokens, d_tokens) + grads[:4] + tuple(item[0] for item in grads[4:])


def solution(mesh):
    parts = Mesh(mesh.devices.reshape(4, 2, 4, 4), ("x", "c", "z", "y"))
    every = ("x", "c", "z", "y")
    group = ("z", "y")
    row, line = P(group, None), P(group)
    return jax.shard_map(
        body,
        mesh=parts,
        in_specs=(P(every, None), P(every)) + (row,) * 4 + (line,) * 9 + (P(every, None),),
        out_specs=(P(every, None),) * 2 + (row,) * 4 + (line,) * 9,
        check_vma=False,
    )
```

```python
import jax
import jax.numpy as jnp
from jax import lax
from jax.experimental import pallas as pl
from jax.experimental.pallas import tpu as pltpu
from jax.sharding import Mesh, PartitionSpec as P

HD = 64
TOK = 128
D = 768
HEADS = 3
WIDTH = HEADS * HD
CHUNK = 512
LOW = jnp.bfloat16
WIDE = jnp.float32


def dot(left, right, dims=((1,), (0,))):
    return lax.dot_general(left, right, (dims, ((), ())), preferred_element_type=WIDE)


def masked(scores, start, place, chunk, block):
    if chunk != block and chunk != 0 and block != 3:
        return scores
    spots = lax.broadcasted_iota(jnp.int32, scores.shape, 0) + chunk * CHUNK
    allowed = None
    if chunk == 0 or block == 3:
        allowed = spots >= start
    if chunk == block:
        causal = spots <= place
        allowed = causal if allowed is None else allowed & causal
    return jnp.where(allowed, scores, -1e30)


def chunk_rows(kv_ref, chunk, low, high):
    return jnp.concatenate(
        [kv_ref[y, chunk * TOK : (chunk + 1) * TOK, low:high] for y in range(4)], axis=0
    )


def forward_kernel(q_ref, kv_ref, bound_ref, att_ref, lse_ref):
    for block in range(4):
        rows = slice(block * TOK, (block + 1) * TOK)
        start = bound_ref[0:1, rows]
        place = bound_ref[1:2, rows]
        for head in range(HEADS):
            cols = slice(head * HD, (head + 1) * HD)
            query = q_ref[rows, cols]
            scores = []
            for chunk in range(block + 1):
                keys = chunk_rows(kv_ref, chunk, head * HD, head * HD + HD)
                scores.append(
                    masked(dot(keys, query, ((1,), (1,))), start, place, chunk, block)
                )
            top = scores[0].max(axis=0, keepdims=True)
            for item in scores[1:]:
                top = jnp.maximum(top, item.max(axis=0, keepdims=True))
            total = jnp.zeros((1, TOK), WIDE)
            summed = jnp.zeros((HD, TOK), WIDE)
            for chunk in range(block + 1):
                weights = jnp.exp(scores[chunk] - top)
                total = total + weights.sum(axis=0, keepdims=True)
                values = chunk_rows(kv_ref, chunk, WIDTH + head * HD, WIDTH + head * HD + HD)
                summed = summed + dot(values, weights.astype(LOW), ((0,), (0,)))
            att_ref[rows, cols] = jnp.transpose(summed / total).astype(LOW)
            lse_ref[head : head + 1, rows] = top + jnp.log(total)


def backward_kernel(q_ref, kv_ref, bound_ref, lse_ref, do_ref, dq_ref, dkv_ref, p_ref, ds_ref):
    for head in range(HEADS):
        cols = slice(head * HD, (head + 1) * HD)
        for block in range(4):
            rows = slice(block * TOK, (block + 1) * TOK)
            start = bound_ref[0:1, rows]
            place = bound_ref[1:2, rows]
            query = q_ref[rows, cols]
            d_out = do_ref[rows, cols]
            lse = lse_ref[head : head + 1, rows]
            delta = jnp.zeros((1, TOK), WIDE)
            probs, d_probs = [], []
            for chunk in range(block + 1):
                keys = chunk_rows(kv_ref, chunk, head * HD, head * HD + HD)
                scores = masked(dot(keys, query, ((1,), (1,))), start, place, chunk, block)
                prob = jnp.exp(scores - lse)
                values = chunk_rows(kv_ref, chunk, WIDTH + head * HD, WIDTH + head * HD + HD)
                d_prob = dot(values, d_out, ((1,), (1,)))
                delta = delta + (prob * d_prob).sum(axis=0, keepdims=True)
                p_ref[chunk * CHUNK : (chunk + 1) * CHUNK, rows] = prob.astype(LOW)
                probs.append(prob)
                d_probs.append(d_prob)
            d_query = jnp.zeros((HD, TOK), WIDE)
            for chunk in range(block + 1):
                d_score = (probs[chunk] * (d_probs[chunk] - delta)).astype(LOW)
                ds_ref[chunk * CHUNK : (chunk + 1) * CHUNK, rows] = d_score
                keys = chunk_rows(kv_ref, chunk, head * HD, head * HD + HD)
                d_query = d_query + dot(keys, d_score, ((0,), (0,)))
            dq_ref[rows, cols] = (jnp.transpose(d_query) * (HD**-0.5)).astype(LOW)
        for chunk in range(4):
            spots = slice(chunk * CHUNK, (chunk + 1) * CHUNK)
            later = slice(chunk * TOK, 4 * TOK)
            d_keys = dot(ds_ref[spots, later], q_ref[later, cols]).astype(LOW)
            d_values = dot(p_ref[spots, later], do_ref[later, cols]).astype(LOW)
            for y in range(4):
                part = slice(y * TOK, (y + 1) * TOK)
                place_rows = slice(chunk * TOK, (chunk + 1) * TOK)
                dkv_ref[y, place_rows, cols] = d_keys[part]
                dkv_ref[y, place_rows, WIDTH + head * HD : WIDTH + head * HD + HD] = d_values[part]


def ffn_kernel(
    own_ref,
    early_ref,
    att_ref,
    gathered_ref,
    up_ref,
    plain_ref,
    wide_ref,
    bias_ref,
    middle_ref,
    normed_hbm,
    act_hbm,
    d_up_hbm,
    d_normed_ref,
    out_hbm,
    sums_ref,
    mid_scr,
    up_scr,
    down_scr,
    cot_scr,
    normed_ref,
    act_ref,
    d_up_ref,
    out_ref,
    sems,
):
    copies = [
        pltpu.make_async_copy(source, target, sems.at[index])
        for index, (source, target) in enumerate(
            (
                (normed_ref, normed_hbm),
                (act_ref, act_hbm),
                (d_up_ref, d_up_hbm),
                (out_ref, out_hbm),
            )
        )
    ]
    for z in range(4):
        for y in range(4):
            row = (4 * z + y) * 48
            up_scr[row : row + 48] = up_ref[y, 48 * z : 48 * z + 48]
        down_scr[192 * z : 192 * z + 192] = plain_ref[z, 0:192]
        cot_scr[TOK * z : TOK * z + TOK] = gathered_ref[z, 0:TOK]
        mid_scr[TOK * z : TOK * z + TOK] = early_ref[z, 0:TOK].astype(WIDE)
    middle = mid_scr[...] + wide_ref[2:3, :]
    for z in range(4):
        middle = middle + dot(att_ref[z], gathered_ref[z, TOK : TOK + 192])
    mid_scr[...] = middle
    middle_ref[...] = mid_scr[pl.ds(pl.multiple_of(own_ref[0] * TOK, TOK), TOK), :]
    average = jnp.mean(middle, axis=-1, keepdims=True)
    centered = middle - average
    variance = jnp.mean(centered * centered, axis=-1, keepdims=True)
    hat = centered * lax.rsqrt(variance + 1e-05)
    normed = (hat * wide_ref[6:7, :] + wide_ref[7:8, :]).astype(LOW)
    normed_ref[...] = normed
    copies[0].start()
    upward = dot(normed, up_scr[...]) + bias_ref[...]
    root = 0.7978845608028654
    square = upward * upward
    bend = jnp.tanh(root * (upward + 0.044715 * (square * upward)))
    level = 0.5 * (1.0 + bend)
    activated = (upward * level).astype(LOW)
    act_ref[...] = activated
    copies[1].start()
    out_ref[...] = dot(activated, down_scr[...]).astype(LOW)
    copies[3].start()
    slope = level + 0.5 * upward * (1.0 - bend * bend) * (root * (1.0 + 0.134145 * square))
    d_act = dot(cot_scr[...], down_scr[...], ((1,), (1,)))
    d_upward = (d_act * slope).astype(LOW)
    d_up_ref[...] = d_upward
    copies[2].start()
    d_normed = dot(d_upward, up_scr[...], ((1,), (1,)))
    d_normed_ref[...] = d_normed.astype(LOW)
    sums_ref[0:1, :] = jnp.sum(d_normed * hat, axis=0, keepdims=True)
    sums_ref[1:2, :] = jnp.sum(d_normed, axis=0, keepdims=True)
    sums_ref[2:3, :] = jnp.sum(d_upward.astype(WIDE), axis=0, keepdims=True)
    sums_ref[3:8, :] = jnp.zeros((5, D), WIDE)
    for copy in copies:
        copy.wait()


def pack_kernel(
    tokens_hbm,
    qkv_hbm,
    up_hbm,
    down_hbm,
    proj_hbm,
    short_ref,
    hidden_ref,
    seg_ref,
    out_ref,
    plain_ref,
    tokens_ref,
    qkv_ref,
    up_ref,
    sems,
):
    pairs = (
        (tokens_hbm, tokens_ref),
        (qkv_hbm, qkv_ref),
        (up_hbm, up_ref),
        (down_hbm, plain_ref.at[pl.ds(0, 192)]),
        (proj_hbm, plain_ref.at[pl.ds(192, 48)]),
    )
    copies = [
        pltpu.make_async_copy(source, target, sems.at[index])
        for index, (source, target) in enumerate(pairs)
    ]
    for copy in copies:
        copy.start()
    seg = seg_ref[...]
    count_one = jnp.sum((seg <= 0).astype(WIDE), axis=1, keepdims=True)
    count_two = jnp.sum((seg <= 1).astype(WIDE), axis=1, keepdims=True)
    spot = lax.broadcasted_iota(jnp.int32, (1, 192), 1)
    counts = jnp.where(spot == 0, count_one, jnp.where(spot == 1, count_two, 0.0))
    side = jnp.concatenate(
        [
            jnp.concatenate(
                [short_ref[...].astype(WIDE), jnp.zeros((8, 144), WIDE)], axis=1
            ),
            jnp.concatenate(
                [hidden_ref[...].astype(WIDE), jnp.zeros((4, 144), WIDE)], axis=1
            ),
            counts,
            jnp.concatenate([seg.astype(WIDE), jnp.zeros((1, 64), WIDE)], axis=1),
            jnp.zeros((34, 192), WIDE),
        ],
        axis=0,
    ).astype(LOW)
    for copy in copies:
        copy.wait()
    for part in range(4):
        out_ref[part, 0:TOK, :] = tokens_ref[...]
        for kind in range(3):
            out_ref[part, TOK : TOK + 48, kind * WIDTH : (kind + 1) * WIDTH] = qkv_ref[
                :, kind * D + part * WIDTH : kind * D + (part + 1) * WIDTH
            ]
        out_ref[part, TOK : TOK + 48, 3 * WIDTH : D] = side
        out_ref[part, TOK + 48 : TOK + 96, :] = up_ref[:, part * D : (part + 1) * D]


def unpack_kernel(core_ref, mine_ref, theirs_ref, qkv_ref, out_ref, up_ref, down_ref, *line_refs):
    first = core_ref[0] == 0
    half = D // 2
    short = jnp.zeros((12, 48), WIDE)
    for part in range(4):
        mine = mine_ref[part].astype(WIDE)
        theirs = theirs_ref[part].astype(WIDE)
        sides = (jnp.where(first, mine, theirs), jnp.where(first, theirs, mine))
        rows = slice(12 * part, 12 * part + 12)
        for core in range(2):
            side = sides[core]
            cols = slice(core * half, (core + 1) * half)
            down_ref[part * 48 : (part + 1) * 48, cols] = side[96:144]
            out_ref[rows, cols] = side[144:156]
            for quarter in range(4):
                low = quarter * D + core * half
                up_ref[rows, low : low + half] = side[24 * quarter : 24 * quarter + 12]
                block = side[24 * quarter + 12 : 24 * quarter + 24]
                low = quarter * WIDTH
                if core == 0:
                    qkv_ref[rows, low : low + WIDTH] = block[:, :WIDTH]
                    qkv_ref[rows, D + low : D + low + WIDTH] = block[:, WIDTH:]
                else:
                    qkv_ref[rows, 2 * D + low : 2 * D + low + WIDTH] = block[:, :WIDTH]
                    if part == 0:
                        short = short + block[:, WIDTH : WIDTH + 48]
    hidden = jnp.concatenate([short[2 + i : 3 + i] for i in range(4)], axis=1)
    lines = [short[i : i + 1] for i in (0, 1, 6)] + [hidden]
    lines += [short[i : i + 1] for i in range(7, 12)]
    for ref, value in zip(line_refs, lines):
        ref[...] = value


VMEM = pl.BlockSpec(memory_space=pltpu.VMEM)
FAR = pl.BlockSpec(memory_space=pltpu.HBM)
PARAMS = pltpu.CompilerParams(vmem_limit_bytes=48 * 1024 * 1024)


def attend_forward(query, kv, bounds):
    return pl.pallas_call(
        forward_kernel,
        out_shape=(
            jax.ShapeDtypeStruct((4 * TOK, WIDTH), LOW),
            jax.ShapeDtypeStruct((8, 4 * TOK), WIDE),
        ),
        in_specs=[VMEM] * 3,
        out_specs=(VMEM, VMEM),
        compiler_params=PARAMS,
        cost_estimate=pl.CostEstimate(
            flops=1_000_000_000, bytes_accessed=4_000_000, transcendentals=2_000_000
        ),
    )(query, kv, bounds)


def attend_backward(query, kv, bounds, lse, d_out):
    return pl.pallas_call(
        backward_kernel,
        out_shape=(
            jax.ShapeDtypeStruct((4 * TOK, WIDTH), LOW),
            jax.ShapeDtypeStruct((4, 4 * TOK, 2 * WIDTH), LOW),
        ),
        in_specs=[VMEM] * 5,
        out_specs=(VMEM, VMEM),
        scratch_shapes=[
            pltpu.VMEM((4 * CHUNK, 4 * TOK), LOW),
            pltpu.VMEM((4 * CHUNK, 4 * TOK), LOW),
        ],
        compiler_params=PARAMS,
        cost_estimate=pl.CostEstimate(
            flops=2_500_000_000, bytes_accessed=6_000_000, transcendentals=2_000_000
        ),
    )(query, kv, bounds, lse, d_out)


def feed_forward(*parts):
    return pl.pallas_call(
        ffn_kernel,
        out_shape=(
            jax.ShapeDtypeStruct((TOK, D), WIDE),
            jax.ShapeDtypeStruct((4 * TOK, D), LOW),
            jax.ShapeDtypeStruct((4 * TOK, D), LOW),
            jax.ShapeDtypeStruct((4 * TOK, D), LOW),
            jax.ShapeDtypeStruct((4 * TOK, D), LOW),
            jax.ShapeDtypeStruct((4 * TOK, D), LOW),
            jax.ShapeDtypeStruct((8, D), WIDE),
        ),
        in_specs=[pl.BlockSpec(memory_space=pltpu.SMEM)] + [VMEM] * 7,
        out_specs=(VMEM, FAR, FAR, FAR, VMEM, FAR, VMEM),
        scratch_shapes=[
            pltpu.VMEM((4 * TOK, D), WIDE),
            pltpu.VMEM((D, D), LOW),
            pltpu.VMEM((D, D), LOW),
            pltpu.VMEM((4 * TOK, D), LOW),
            pltpu.VMEM((4 * TOK, D), LOW),
            pltpu.VMEM((4 * TOK, D), LOW),
            pltpu.VMEM((4 * TOK, D), LOW),
            pltpu.VMEM((4 * TOK, D), LOW),
            pltpu.SemaphoreType.DMA((4,)),
        ],
        compiler_params=PARAMS,
        cost_estimate=pl.CostEstimate(
            flops=4_000_000_000, bytes_accessed=12_000_000, transcendentals=400_000
        ),
    )(*parts)


def pack(*parts):
    return pl.pallas_call(
        pack_kernel,
        out_shape=(
            jax.ShapeDtypeStruct((4, TOK + 96, D), LOW),
            jax.ShapeDtypeStruct((240, D), LOW),
        ),
        in_specs=[FAR] * 5 + [VMEM] * 3,
        out_specs=(VMEM, VMEM),
        scratch_shapes=[
            pltpu.VMEM((TOK, D), LOW),
            pltpu.VMEM((48, 3 * D), LOW),
            pltpu.VMEM((48, 4 * D), LOW),
            pltpu.SemaphoreType.DMA((5,)),
        ],
        compiler_params=PARAMS,
        cost_estimate=pl.CostEstimate(
            flops=1_000_000, bytes_accessed=2_500_000, transcendentals=0
        ),
    )(*parts)


def unpack(core, mine, theirs):
    return pl.pallas_call(
        unpack_kernel,
        out_shape=tuple(
            jax.ShapeDtypeStruct(shape, WIDE)
            for shape in ((48, 3 * D), (48, D), (48, 4 * D), (192, D))
            + ((1, 48),) * 3
            + ((1, 192),)
            + ((1, 48),) * 5
        ),
        in_specs=[pl.BlockSpec(memory_space=pltpu.SMEM), VMEM, VMEM],
        out_specs=(VMEM,) * 13,
        compiler_params=PARAMS,
        cost_estimate=pl.CostEstimate(
            flops=1_000_000, bytes_accessed=3_500_000, transcendentals=0
        ),
    )(core, mine, theirs)


def norm_parts(values):
    average = jnp.mean(values, axis=-1, keepdims=True)
    centered = values - average
    variance = jnp.mean(centered * centered, axis=-1, keepdims=True)
    inverse = lax.rsqrt(variance + 1e-05)
    return centered * inverse, inverse


def norm_back(hat, inverse, gain, grad):
    scaled = grad * gain
    mean_one = jnp.mean(scaled, axis=-1, keepdims=True)
    mean_two = jnp.mean(scaled * hat, axis=-1, keepdims=True)
    return inverse * (scaled - mean_one - hat * mean_two)


def swap(value, axis):
    return lax.all_to_all(value, axis, 0, 0, tiled=True)


def share(value, axis):
    return swap(jnp.broadcast_to(value[None], (4,) + value.shape), axis)


def total(value):
    return jnp.sum(value.astype(WIDE), axis=0)


def other_core(value):
    return lax.ppermute(value, "c", [(0, 1), (1, 0)])


def body(
    tokens,
    segments,
    w_qkv,
    w_out,
    w_up,
    w_down,
    b_query,
    b_value,
    b_out,
    b_up,
    b_down,
    ln1_gain,
    ln1_shift,
    ln2_gain,
    ln2_shift,
    cotangent,
):
    ix, ic, iz, iy = (lax.axis_index(name) for name in ("x", "c", "z", "y"))
    first_doc = 3 * (2 * ix + ic)
    half = D // 2

    def lanes(value, core):
        return lax.dynamic_slice_in_dim(value, core * half, half, value.ndim - 1)

    short = jnp.stack(
        [b_query, b_value, b_out, b_down, ln1_gain, ln1_shift, ln2_gain, ln2_shift]
    )
    early, plain = pack(
        tokens,
        w_qkv,
        w_up,
        w_down,
        w_out,
        short,
        b_up.reshape(4, 48),
        (segments - first_doc)[None],
    )
    early = swap(early, "z")
    token_all = early[:, :TOK].reshape(4 * TOK, D)
    seg_all = early[:, TOK + 13, 576:704].astype(jnp.int32)
    early_all = share(early[:, TOK : TOK + 48, :640], "y").swapaxes(0, 1)
    qkv_part = early_all[:, :, :, :576].reshape(D, 3 * WIDTH)
    small_all = early_all[:, :, :16, 576:624].astype(WIDE)
    total_counts = jnp.sum(small_all[:, :, 12, :2], axis=(0, 1)).astype(jnp.int32)
    wide = small_all.reshape(16, 16, 48)[:, :8].swapaxes(0, 1).reshape(8, D)
    bias_out, bias_down, gain_one, shift_one, gain_two, shift_two = (
        wide[index] for index in range(2, 8)
    )
    own = lax.dynamic_index_in_dim(small_all, iz, 0, keepdims=False)
    bias_query = own[:, 0].reshape(WIDTH)
    bias_value = own[:, 1].reshape(WIDTH)
    bias_up = own[:, 8:12].reshape(D)

    plain = lax.all_gather(plain, "y")
    gathered = lax.all_gather(
        jnp.concatenate([cotangent, plain[:, 192:].reshape(192, D)], axis=0), "z"
    )
    up_rows, gathered = lax.optimization_barrier((early[:, TOK + 48 :], gathered))
    up_part = lax.all_gather(up_rows.reshape(192, D), "y")
    out_rows = lax.dynamic_index_in_dim(gathered, iz, 0, keepdims=False)[TOK:]
    cot_all = gathered[:, :TOK].reshape(4 * TOK, D)

    inputs = token_all.astype(WIDE)
    start = jnp.where(
        seg_all <= 0, 0, jnp.where(seg_all <= 1, total_counts[0], total_counts[1])
    )
    place = (
        4 * TOK * jnp.arange(4, dtype=jnp.int32)[:, None]
        + TOK * iy
        + jnp.arange(TOK, dtype=jnp.int32)[None, :]
    )
    bounds = jnp.concatenate(
        [start.reshape(1, 4 * TOK), place.reshape(1, 4 * TOK), jnp.zeros((6, 4 * TOK), jnp.int32)]
    )

    hat_one, inverse_one = norm_parts(inputs)
    normed_one = (hat_one * gain_one + shift_one).astype(LOW)
    qkv = dot(normed_one, qkv_part)
    query = ((qkv[:, :WIDTH] + bias_query).astype(LOW) * (HD**-0.5)).astype(LOW)
    kv = jnp.concatenate(
        [qkv[:, WIDTH : 2 * WIDTH], qkv[:, 2 * WIDTH :] + bias_value], axis=1
    ).astype(LOW)
    kv_all = share(kv, "y")
    att_part, lse = attend_forward(query, kv_all, bounds)
    att_all = share(att_part, "z")

    middle, normed_two, activated, d_upward, d_normed, out_part, sums = feed_forward(
        iz.astype(jnp.int32)[None], early, att_all, gathered, up_part, plain, wide, bias_up[None]
    )
    d_gain_two, d_shift_two, d_bias_up = sums[0], sums[1], sums[2]
    d_normed = total(swap(d_normed.reshape(4, TOK, D), "z"))
    own_rows = iz * TOK

    def mine(value):
        return lax.dynamic_slice_in_dim(value, own_rows, TOK, 0)

    hat_two, inverse_two = norm_parts(middle)
    d_middle = cotangent.astype(WIDE) + norm_back(hat_two, inverse_two, gain_two, d_normed)
    d_branch = d_middle.astype(LOW)
    branch_all = share(d_branch, "z").reshape(4 * TOK, D)
    d_attended = dot(branch_all, out_rows, ((1,), (1,))).astype(LOW)

    d_query, d_kv = attend_backward(query, kv_all, bounds, lse, d_attended)

    d_kv, late_up, late_act, late_att = lax.optimization_barrier(
        (d_kv, d_upward, activated, att_part)
    )
    d_up = dot(normed_two, late_up, ((0,), (0,))).astype(LOW)
    d_down = dot(late_act, cot_all, ((0,), (0,))).astype(LOW)
    d_out = dot(late_att, branch_all, ((0,), (0,))).astype(LOW)
    first = jnp.concatenate(
        [
            d_up.reshape(4, 4, 4, 12, 2, half).transpose(2, 4, 1, 0, 3, 5).reshape(4, 2, 4, 48, half),
            d_down.reshape(4, 4, 48, 2, half).transpose(1, 3, 0, 2, 4),
            d_out.reshape(4, 4, 12, 2, half).transpose(1, 3, 0, 2, 4),
            jnp.zeros((4, 2, 4, 4, half), LOW),
        ],
        axis=3,
    )
    first = lax.psum_scatter(first.reshape(8, 448, half), ("x", "c"), scatter_dimension=0)
    d_kv = total(swap(d_kv, "y")).astype(LOW)
    d_qkv = jnp.concatenate([d_query, d_kv], axis=1)
    d_normed = dot(d_qkv, qkv_part, ((1,), (1,)))
    d_gain_one = jnp.sum(d_normed * hat_one, axis=0)
    d_shift_one = jnp.sum(d_normed, axis=0)
    d_qkv_w = dot(normed_one, d_qkv, ((0,), (0,))).astype(LOW)

    d_qkv_sum = jnp.sum(d_qkv.astype(WIDE), axis=0)
    here = (jnp.arange(4) == iz).astype(WIDE)[:, None, None, None]
    of_z = jnp.concatenate(
        [
            d_qkv_sum[:WIDTH].reshape(4, 1, 48),
            d_qkv_sum[2 * WIDTH :].reshape(4, 1, 48),
            d_bias_up.reshape(4, 4, 48),
        ],
        axis=1,
    )
    of_all = jnp.stack(
        [
            jnp.sum(d_branch.astype(WIDE), axis=0),
            jnp.sum(cotangent.astype(WIDE), axis=0),
            d_gain_one,
            d_shift_one,
            d_gain_two,
            d_shift_two,
        ]
    )
    smalls = jnp.concatenate(
        [
            (of_z[None] * here).reshape(16, 6, 48),
            of_all.reshape(6, 16, 48).swapaxes(0, 1),
        ],
        axis=1,
    )
    smalls = jnp.pad(smalls.astype(LOW), ((0, 0), (0, 36), (0, 144)))
    second = jnp.concatenate([d_qkv_w.reshape(16, 48, 576), smalls], axis=2)
    got = other_core(lanes(second, 1 - ic))
    second = (lanes(second, ic).astype(WIDE) + got.astype(WIDE)).astype(LOW)
    second, late_normed = lax.optimization_barrier((second, d_normed))
    second = second.reshape(4, 4, 48, half).swapaxes(0, 1).reshape(4, 192, half)
    second = jnp.concatenate([first.reshape(4, 112, half), second], axis=1)
    second = total(swap(second, "y")).astype(LOW)
    last = jnp.concatenate([late_normed.astype(LOW), out_part], axis=1).reshape(4, TOK, 2 * D)
    last = lax.psum_scatter(last, "z", scatter_dimension=0).astype(WIDE)
    d_normed = last[:, :D]
    out_tokens = (middle + last[:, D:] + bias_down).astype(LOW)
    d_tokens = (
        d_middle + norm_back(mine(hat_one), mine(inverse_one), gain_one, d_normed)
    ).astype(LOW)

    here_x = (jnp.arange(4) == ix)[:, None, None, None]
    joint = jnp.concatenate(
        [
            jnp.where(here_x, second[:48].reshape(1, 4, 12, half), jnp.zeros((), LOW)),
            second[112:].reshape(4, 4, 12, half).swapaxes(0, 1),
        ],
        axis=2,
    ).reshape(16, 24, half)
    joint = total(swap(joint, ("x", "z")).reshape(4, 4, 24, half)).astype(LOW)
    rows = second[48:112]
    whole = share(jnp.concatenate([joint.reshape(96, half), rows], axis=0), "x")
    theirs = other_core(whole)
    grads = unpack(ic.astype(jnp.int32)[None], whole, theirs)
    return (out_tokens, d_tokens) + grads[:4] + tuple(item[0] for item in grads[4:])


def solution(mesh):
    parts = Mesh(mesh.devices.reshape(4, 2, 4, 4), ("x", "c", "z", "y"))
    every = ("x", "c", "z", "y")
    group = ("z", "y")
    row, line = P(group, None), P(group)
    return jax.shard_map(
        body,
        mesh=parts,
        in_specs=(P(every, None), P(every)) + (row,) * 4 + (line,) * 9 + (P(every, None),),
        out_specs=(P(every, None),) * 2 + (row,) * 4 + (line,) * 9,
        check_vma=False,
    )
```

```python
import jax
import jax.numpy as jnp
from jax import lax
from jax.experimental import pallas as pl
from jax.experimental.pallas import tpu as pltpu
from jax.sharding import Mesh, PartitionSpec as P

HD = 64
TOK = 128
D = 768
HEADS = 3
WIDTH = HEADS * HD
CHUNK = 512
LOW = jnp.bfloat16
WIDE = jnp.float32


def dot(left, right, dims=((1,), (0,))):
    return lax.dot_general(left, right, (dims, ((), ())), preferred_element_type=WIDE)


def masked(scores, start, place, chunk, block):
    if chunk != block and chunk != 0 and block != 3:
        return scores
    spots = lax.broadcasted_iota(jnp.int32, scores.shape, 0) + chunk * CHUNK
    allowed = None
    if chunk == 0 or block == 3:
        allowed = spots >= start
    if chunk == block:
        causal = spots <= place
        allowed = causal if allowed is None else allowed & causal
    return jnp.where(allowed, scores, -1e30)


def chunk_rows(kv_ref, chunk, low, high):
    return jnp.concatenate(
        [kv_ref[y, chunk * TOK : (chunk + 1) * TOK, low:high] for y in range(4)], axis=0
    )


def forward_kernel(q_ref, kv_ref, bound_ref, att_ref, lse_ref):
    for block in range(4):
        rows = slice(block * TOK, (block + 1) * TOK)
        start = bound_ref[0:1, rows]
        place = bound_ref[1:2, rows]
        for head in range(HEADS):
            cols = slice(head * HD, (head + 1) * HD)
            query = q_ref[rows, cols]
            scores = []
            for chunk in range(block + 1):
                keys = chunk_rows(kv_ref, chunk, head * HD, head * HD + HD)
                scores.append(
                    masked(dot(keys, query, ((1,), (1,))), start, place, chunk, block)
                )
            top = scores[0].max(axis=0, keepdims=True)
            for item in scores[1:]:
                top = jnp.maximum(top, item.max(axis=0, keepdims=True))
            total = jnp.zeros((1, TOK), WIDE)
            summed = jnp.zeros((HD, TOK), WIDE)
            for chunk in range(block + 1):
                weights = jnp.exp(scores[chunk] - top)
                total = total + weights.sum(axis=0, keepdims=True)
                values = chunk_rows(kv_ref, chunk, WIDTH + head * HD, WIDTH + head * HD + HD)
                summed = summed + dot(values, weights.astype(LOW), ((0,), (0,)))
            att_ref[rows, cols] = jnp.transpose(summed / total).astype(LOW)
            lse_ref[head : head + 1, rows] = top + jnp.log(total)


def backward_kernel(q_ref, kv_ref, bound_ref, lse_ref, do_ref, dq_ref, dkv_ref, p_ref, ds_ref):
    for head in range(HEADS):
        cols = slice(head * HD, (head + 1) * HD)
        for block in range(4):
            rows = slice(block * TOK, (block + 1) * TOK)
            start = bound_ref[0:1, rows]
            place = bound_ref[1:2, rows]
            query = q_ref[rows, cols]
            d_out = do_ref[rows, cols]
            lse = lse_ref[head : head + 1, rows]
            delta = jnp.zeros((1, TOK), WIDE)
            probs, d_probs = [], []
            for chunk in range(block + 1):
                keys = chunk_rows(kv_ref, chunk, head * HD, head * HD + HD)
                scores = masked(dot(keys, query, ((1,), (1,))), start, place, chunk, block)
                prob = jnp.exp(scores - lse)
                values = chunk_rows(kv_ref, chunk, WIDTH + head * HD, WIDTH + head * HD + HD)
                d_prob = dot(values, d_out, ((1,), (1,)))
                delta = delta + (prob * d_prob).sum(axis=0, keepdims=True)
                p_ref[chunk * CHUNK : (chunk + 1) * CHUNK, rows] = prob.astype(LOW)
                probs.append(prob)
                d_probs.append(d_prob)
            d_query = jnp.zeros((HD, TOK), WIDE)
            for chunk in range(block + 1):
                d_score = (probs[chunk] * (d_probs[chunk] - delta)).astype(LOW)
                ds_ref[chunk * CHUNK : (chunk + 1) * CHUNK, rows] = d_score
                keys = chunk_rows(kv_ref, chunk, head * HD, head * HD + HD)
                d_query = d_query + dot(keys, d_score, ((0,), (0,)))
            dq_ref[rows, cols] = (jnp.transpose(d_query) * (HD**-0.5)).astype(LOW)
        for chunk in range(4):
            spots = slice(chunk * CHUNK, (chunk + 1) * CHUNK)
            later = slice(chunk * TOK, 4 * TOK)
            d_keys = dot(ds_ref[spots, later], q_ref[later, cols]).astype(LOW)
            d_values = dot(p_ref[spots, later], do_ref[later, cols]).astype(LOW)
            for y in range(4):
                part = slice(y * TOK, (y + 1) * TOK)
                place_rows = slice(chunk * TOK, (chunk + 1) * TOK)
                dkv_ref[y, place_rows, cols] = d_keys[part]
                dkv_ref[y, place_rows, WIDTH + head * HD : WIDTH + head * HD + HD] = d_values[part]


def ffn_kernel(
    own_ref,
    early_ref,
    att_ref,
    gathered_ref,
    up_ref,
    plain_ref,
    wide_ref,
    bias_ref,
    middle_ref,
    normed_hbm,
    act_hbm,
    d_up_hbm,
    d_normed_ref,
    out_hbm,
    sums_ref,
    mid_scr,
    up_scr,
    down_scr,
    cot_scr,
    normed_ref,
    act_ref,
    d_up_ref,
    out_ref,
    sems,
):
    copies = [
        pltpu.make_async_copy(source, target, sems.at[index])
        for index, (source, target) in enumerate(
            (
                (normed_ref, normed_hbm),
                (act_ref, act_hbm),
                (d_up_ref, d_up_hbm),
                (out_ref, out_hbm),
            )
        )
    ]
    for z in range(4):
        for y in range(4):
            row = (4 * z + y) * 48
            up_scr[row : row + 48] = up_ref[y, 48 * z : 48 * z + 48]
        down_scr[192 * z : 192 * z + 192] = plain_ref[z, 0:192]
        cot_scr[TOK * z : TOK * z + TOK] = gathered_ref[z, 0:TOK]
        mid_scr[TOK * z : TOK * z + TOK] = early_ref[z, 0:TOK].astype(WIDE)
    middle = mid_scr[...] + wide_ref[2:3, :]
    for z in range(4):
        middle = middle + dot(att_ref[z], gathered_ref[z, TOK : TOK + 192])
    mid_scr[...] = middle
    middle_ref[...] = mid_scr[pl.ds(pl.multiple_of(own_ref[0] * TOK, TOK), TOK), :]
    average = jnp.mean(middle, axis=-1, keepdims=True)
    centered = middle - average
    variance = jnp.mean(centered * centered, axis=-1, keepdims=True)
    hat = centered * lax.rsqrt(variance + 1e-05)
    normed = (hat * wide_ref[6:7, :] + wide_ref[7:8, :]).astype(LOW)
    normed_ref[...] = normed
    copies[0].start()
    upward = dot(normed, up_scr[...]) + bias_ref[...]
    root = 0.7978845608028654
    square = upward * upward
    bend = jnp.tanh(root * (upward + 0.044715 * (square * upward)))
    level = 0.5 * (1.0 + bend)
    activated = (upward * level).astype(LOW)
    act_ref[...] = activated
    copies[1].start()
    out_ref[...] = dot(activated, down_scr[...]).astype(LOW)
    copies[3].start()
    slope = level + 0.5 * upward * (1.0 - bend * bend) * (root * (1.0 + 0.134145 * square))
    d_act = dot(cot_scr[...], down_scr[...], ((1,), (1,)))
    d_upward = (d_act * slope).astype(LOW)
    d_up_ref[...] = d_upward
    copies[2].start()
    d_normed = dot(d_upward, up_scr[...], ((1,), (1,)))
    d_normed_ref[...] = d_normed.astype(LOW)
    sums_ref[0:1, :] = jnp.sum(d_normed * hat, axis=0, keepdims=True)
    sums_ref[1:2, :] = jnp.sum(d_normed, axis=0, keepdims=True)
    sums_ref[2:3, :] = jnp.sum(d_upward.astype(WIDE), axis=0, keepdims=True)
    sums_ref[3:8, :] = jnp.zeros((5, D), WIDE)
    for copy in copies:
        copy.wait()


def grad_kernel(normed_ref, d_up_ref, act_ref, gathered_ref, att_ref, branch_ref, out_ref, cot_scr):
    half = D // 2
    for z in range(4):
        cot_scr[TOK * z : TOK * z + TOK] = gathered_ref[z, 0:TOK]
    up = dot(normed_ref[...], d_up_ref[...], ((0,), (0,))).astype(LOW)
    down = dot(act_ref[...], cot_scr[...], ((0,), (0,))).astype(LOW)
    proj = dot(att_ref[...], branch_ref[...], ((0,), (0,))).astype(LOW)
    blank = jnp.zeros((16, half), LOW)
    for x in range(4):
        for core in range(2):
            cols = slice(core * half, core * half + half)
            slot = 2 * x + core
            for y in range(4):
                base = TOK * y
                for z in range(4):
                    row = (4 * z + y) * 48 + 16 * x
                    out_ref[slot, base + 16 * z : base + 16 * z + 16] = (
                        up[row : row + 16, cols] if x < 3 else blank
                    )
                row = 192 * y + 48 * x
                out_ref[slot, base + 64 : base + 112] = down[row : row + 48, cols]
                row = 48 * y + 16 * x
                out_ref[slot, base + 112 : base + 128] = (
                    proj[row : row + 16, cols] if x < 3 else blank
                )


def pack_kernel(
    tokens_hbm,
    qkv_hbm,
    up_hbm,
    down_hbm,
    proj_hbm,
    short_ref,
    hidden_ref,
    seg_ref,
    out_ref,
    plain_ref,
    tokens_ref,
    qkv_ref,
    up_ref,
    sems,
):
    pairs = (
        (tokens_hbm, tokens_ref),
        (qkv_hbm, qkv_ref),
        (up_hbm, up_ref),
        (down_hbm, plain_ref.at[pl.ds(0, 192)]),
        (proj_hbm, plain_ref.at[pl.ds(192, 48)]),
    )
    copies = [
        pltpu.make_async_copy(source, target, sems.at[index])
        for index, (source, target) in enumerate(pairs)
    ]
    for copy in copies:
        copy.start()
    seg = seg_ref[...]
    count_one = jnp.sum((seg <= 0).astype(WIDE), axis=1, keepdims=True)
    count_two = jnp.sum((seg <= 1).astype(WIDE), axis=1, keepdims=True)
    spot = lax.broadcasted_iota(jnp.int32, (1, 192), 1)
    counts = jnp.where(spot == 0, count_one, jnp.where(spot == 1, count_two, 0.0))
    side = jnp.concatenate(
        [
            jnp.concatenate(
                [short_ref[...].astype(WIDE), jnp.zeros((8, 144), WIDE)], axis=1
            ),
            jnp.concatenate(
                [hidden_ref[...].astype(WIDE), jnp.zeros((4, 144), WIDE)], axis=1
            ),
            counts,
            jnp.concatenate([seg.astype(WIDE), jnp.zeros((1, 64), WIDE)], axis=1),
            jnp.zeros((34, 192), WIDE),
        ],
        axis=0,
    ).astype(LOW)
    for copy in copies:
        copy.wait()
    for part in range(4):
        out_ref[part, 0:TOK, :] = tokens_ref[...]
        for kind in range(3):
            out_ref[part, TOK : TOK + 48, kind * WIDTH : (kind + 1) * WIDTH] = qkv_ref[
                :, kind * D + part * WIDTH : kind * D + (part + 1) * WIDTH
            ]
        out_ref[part, TOK : TOK + 48, 3 * WIDTH : D] = side
        out_ref[part, TOK + 48 : TOK + 96, :] = up_ref[:, part * D : (part + 1) * D]


def unpack_kernel(core_ref, mine_ref, theirs_ref, qkv_ref, out_ref, up_ref, down_ref, *line_refs):
    first = core_ref[0] == 0
    half = D // 2
    short = jnp.zeros((12, 48), WIDE)
    for part in range(4):
        mine = mine_ref[part].astype(WIDE)
        theirs = theirs_ref[part].astype(WIDE)
        sides = (jnp.where(first, mine, theirs), jnp.where(first, theirs, mine))
        rows = slice(16 * part, 16 * part + 16)
        for core in range(2):
            side = sides[core]
            cols = slice(core * half, (core + 1) * half)
            down_ref[part * 48 : (part + 1) * 48, cols] = side[TOK : TOK + 48]
            if part == 3:
                continue
            out_ref[rows, cols] = side[TOK + 48 : TOK + 64]
            for quarter in range(4):
                low = quarter * D + core * half
                up_ref[rows, low : low + half] = side[32 * quarter : 32 * quarter + 16]
                block = side[32 * quarter + 16 : 32 * quarter + 32]
                low = quarter * WIDTH
                if core == 0:
                    qkv_ref[rows, low : low + WIDTH] = block[:, :WIDTH]
                    qkv_ref[rows, D + low : D + low + WIDTH] = block[:, WIDTH:]
                else:
                    qkv_ref[rows, 2 * D + low : 2 * D + low + WIDTH] = block[:, :WIDTH]
                    if part == 0:
                        short = short + block[:12, WIDTH : WIDTH + 48]
    hidden = jnp.concatenate([short[2 + i : 3 + i] for i in range(4)], axis=1)
    lines = [short[i : i + 1] for i in (0, 1, 6)] + [hidden]
    lines += [short[i : i + 1] for i in range(7, 12)]
    for ref, value in zip(line_refs, lines):
        ref[...] = value


VMEM = pl.BlockSpec(memory_space=pltpu.VMEM)
FAR = pl.BlockSpec(memory_space=pltpu.HBM)
PARAMS = pltpu.CompilerParams(vmem_limit_bytes=48 * 1024 * 1024)
WHOLE = pltpu.CompilerParams(vmem_limit_bytes=60 * 1024 * 1024)


def attend_forward(query, kv, bounds):
    return pl.pallas_call(
        forward_kernel,
        out_shape=(
            jax.ShapeDtypeStruct((4 * TOK, WIDTH), LOW),
            jax.ShapeDtypeStruct((8, 4 * TOK), WIDE),
        ),
        in_specs=[VMEM] * 3,
        out_specs=(VMEM, VMEM),
        compiler_params=PARAMS,
        cost_estimate=pl.CostEstimate(
            flops=1_000_000_000, bytes_accessed=4_000_000, transcendentals=2_000_000
        ),
    )(query, kv, bounds)


def attend_backward(query, kv, bounds, lse, d_out):
    return pl.pallas_call(
        backward_kernel,
        out_shape=(
            jax.ShapeDtypeStruct((4 * TOK, WIDTH), LOW),
            jax.ShapeDtypeStruct((4, 4 * TOK, 2 * WIDTH), LOW),
        ),
        in_specs=[VMEM] * 5,
        out_specs=(VMEM, VMEM),
        scratch_shapes=[
            pltpu.VMEM((4 * CHUNK, 4 * TOK), LOW),
            pltpu.VMEM((4 * CHUNK, 4 * TOK), LOW),
        ],
        compiler_params=PARAMS,
        cost_estimate=pl.CostEstimate(
            flops=2_500_000_000, bytes_accessed=6_000_000, transcendentals=2_000_000
        ),
    )(query, kv, bounds, lse, d_out)


def feed_forward(*parts):
    return pl.pallas_call(
        ffn_kernel,
        out_shape=(
            jax.ShapeDtypeStruct((TOK, D), WIDE),
            jax.ShapeDtypeStruct((4 * TOK, D), LOW),
            jax.ShapeDtypeStruct((4 * TOK, D), LOW),
            jax.ShapeDtypeStruct((4 * TOK, D), LOW),
            jax.ShapeDtypeStruct((4 * TOK, D), LOW),
            jax.ShapeDtypeStruct((4 * TOK, D), LOW),
            jax.ShapeDtypeStruct((8, D), WIDE),
        ),
        in_specs=[pl.BlockSpec(memory_space=pltpu.SMEM)] + [VMEM] * 7,
        out_specs=(VMEM, FAR, FAR, FAR, VMEM, FAR, VMEM),
        scratch_shapes=[
            pltpu.VMEM((4 * TOK, D), WIDE),
            pltpu.VMEM((D, D), LOW),
            pltpu.VMEM((D, D), LOW),
            pltpu.VMEM((4 * TOK, D), LOW),
            pltpu.VMEM((4 * TOK, D), LOW),
            pltpu.VMEM((4 * TOK, D), LOW),
            pltpu.VMEM((4 * TOK, D), LOW),
            pltpu.VMEM((4 * TOK, D), LOW),
            pltpu.SemaphoreType.DMA((4,)),
        ],
        compiler_params=WHOLE,
        cost_estimate=pl.CostEstimate(
            flops=4_000_000_000, bytes_accessed=12_000_000, transcendentals=400_000
        ),
    )(*parts)


def weight_grads(*parts):
    return pl.pallas_call(
        grad_kernel,
        out_shape=jax.ShapeDtypeStruct((8, 4 * TOK, D // 2), LOW),
        in_specs=[VMEM] * 6,
        out_specs=VMEM,
        scratch_shapes=[pltpu.VMEM((4 * TOK, D), LOW)],
        compiler_params=PARAMS,
        cost_estimate=pl.CostEstimate(
            flops=1_400_000_000, bytes_accessed=9_000_000, transcendentals=0
        ),
    )(*parts)


def pack(*parts):
    return pl.pallas_call(
        pack_kernel,
        out_shape=(
            jax.ShapeDtypeStruct((4, TOK + 96, D), LOW),
            jax.ShapeDtypeStruct((240, D), LOW),
        ),
        in_specs=[FAR] * 5 + [VMEM] * 3,
        out_specs=(VMEM, VMEM),
        scratch_shapes=[
            pltpu.VMEM((TOK, D), LOW),
            pltpu.VMEM((48, 3 * D), LOW),
            pltpu.VMEM((48, 4 * D), LOW),
            pltpu.SemaphoreType.DMA((5,)),
        ],
        compiler_params=WHOLE,
        cost_estimate=pl.CostEstimate(
            flops=1_000_000, bytes_accessed=2_500_000, transcendentals=0
        ),
    )(*parts)


def unpack(core, mine, theirs):
    return pl.pallas_call(
        unpack_kernel,
        out_shape=tuple(
            jax.ShapeDtypeStruct(shape, WIDE)
            for shape in ((48, 3 * D), (48, D), (48, 4 * D), (192, D))
            + ((1, 48),) * 3
            + ((1, 192),)
            + ((1, 48),) * 5
        ),
        in_specs=[pl.BlockSpec(memory_space=pltpu.SMEM), VMEM, VMEM],
        out_specs=(VMEM,) * 13,
        compiler_params=PARAMS,
        cost_estimate=pl.CostEstimate(
            flops=1_000_000, bytes_accessed=3_500_000, transcendentals=0
        ),
    )(core, mine, theirs)


def norm_parts(values):
    average = jnp.mean(values, axis=-1, keepdims=True)
    centered = values - average
    variance = jnp.mean(centered * centered, axis=-1, keepdims=True)
    inverse = lax.rsqrt(variance + 1e-05)
    return centered * inverse, inverse


def norm_back(hat, inverse, gain, grad):
    scaled = grad * gain
    mean_one = jnp.mean(scaled, axis=-1, keepdims=True)
    mean_two = jnp.mean(scaled * hat, axis=-1, keepdims=True)
    return inverse * (scaled - mean_one - hat * mean_two)


def swap(value, axis):
    return lax.all_to_all(value, axis, 0, 0, tiled=True)


def share(value, axis):
    return swap(jnp.broadcast_to(value[None], (4,) + value.shape), axis)


def total(value):
    return jnp.sum(value.astype(WIDE), axis=0)


def other_core(value):
    return lax.ppermute(value, "c", [(0, 1), (1, 0)])


def body(
    tokens,
    segments,
    w_qkv,
    w_out,
    w_up,
    w_down,
    b_query,
    b_value,
    b_out,
    b_up,
    b_down,
    ln1_gain,
    ln1_shift,
    ln2_gain,
    ln2_shift,
    cotangent,
):
    ix, ic, iz, iy = (lax.axis_index(name) for name in ("x", "c", "z", "y"))
    first_doc = 3 * (2 * ix + ic)
    half = D // 2

    def lanes(value, core):
        return lax.dynamic_slice_in_dim(value, core * half, half, value.ndim - 1)

    short = jnp.stack(
        [b_query, b_value, b_out, b_down, ln1_gain, ln1_shift, ln2_gain, ln2_shift]
    )
    early, plain = pack(
        tokens,
        w_qkv,
        w_up,
        w_down,
        w_out,
        short,
        b_up.reshape(4, 48),
        (segments - first_doc)[None],
    )
    early = swap(early, "z")
    token_all = early[:, :TOK].reshape(4 * TOK, D)
    seg_all = early[:, TOK + 13, 576:704].astype(jnp.int32)
    early_all = share(early[:, TOK : TOK + 48, :640], "y").swapaxes(0, 1)
    qkv_part = early_all[:, :, :, :576].reshape(D, 3 * WIDTH)
    small_all = early_all[:, :, :16, 576:624].astype(WIDE)
    total_counts = jnp.sum(small_all[:, :, 12, :2], axis=(0, 1)).astype(jnp.int32)
    wide = small_all.reshape(16, 16, 48)[:, :8].swapaxes(0, 1).reshape(8, D)
    bias_out, bias_down, gain_one, shift_one, gain_two, shift_two = (
        wide[index] for index in range(2, 8)
    )
    own = lax.dynamic_index_in_dim(small_all, iz, 0, keepdims=False)
    bias_query = own[:, 0].reshape(WIDTH)
    bias_value = own[:, 1].reshape(WIDTH)
    bias_up = own[:, 8:12].reshape(D)

    plain = lax.all_gather(plain, "y")
    gathered = lax.all_gather(
        jnp.concatenate([cotangent, plain[:, 192:].reshape(192, D)], axis=0), "z"
    )
    up_rows, gathered = lax.optimization_barrier((early[:, TOK + 48 :], gathered))
    up_part = lax.all_gather(up_rows.reshape(192, D), "y")
    out_rows = lax.dynamic_index_in_dim(gathered, iz, 0, keepdims=False)[TOK:]
    cot_all = gathered[:, :TOK].reshape(4 * TOK, D)

    inputs = token_all.astype(WIDE)
    start = jnp.where(
        seg_all <= 0, 0, jnp.where(seg_all <= 1, total_counts[0], total_counts[1])
    )
    place = (
        4 * TOK * jnp.arange(4, dtype=jnp.int32)[:, None]
        + TOK * iy
        + jnp.arange(TOK, dtype=jnp.int32)[None, :]
    )
    bounds = jnp.concatenate(
        [start.reshape(1, 4 * TOK), place.reshape(1, 4 * TOK), jnp.zeros((6, 4 * TOK), jnp.int32)]
    )

    hat_one, inverse_one = norm_parts(inputs)
    normed_one = (hat_one * gain_one + shift_one).astype(LOW)
    qkv = dot(normed_one, qkv_part)
    query = ((qkv[:, :WIDTH] + bias_query).astype(LOW) * (HD**-0.5)).astype(LOW)
    kv = jnp.concatenate(
        [qkv[:, WIDTH : 2 * WIDTH], qkv[:, 2 * WIDTH :] + bias_value], axis=1
    ).astype(LOW)
    kv_all = share(kv, "y")
    att_part, lse = attend_forward(query, kv_all, bounds)
    att_all = share(att_part, "z")

    middle, normed_two, activated, d_upward, d_normed, out_part, sums = feed_forward(
        iz.astype(jnp.int32)[None], early, att_all, gathered, up_part, plain, wide, bias_up[None]
    )
    d_gain_two, d_shift_two, d_bias_up = sums[0], sums[1], sums[2]
    d_normed = total(swap(d_normed.reshape(4, TOK, D), "z"))
    own_rows = iz * TOK

    def mine(value):
        return lax.dynamic_slice_in_dim(value, own_rows, TOK, 0)

    hat_two, inverse_two = norm_parts(middle)
    d_middle = cotangent.astype(WIDE) + norm_back(hat_two, inverse_two, gain_two, d_normed)
    d_branch = d_middle.astype(LOW)
    branch_all = share(d_branch, "z").reshape(4 * TOK, D)
    d_attended = dot(branch_all, out_rows, ((1,), (1,))).astype(LOW)

    d_query, d_kv = attend_backward(query, kv_all, bounds, lse, d_attended)

    first = weight_grads(normed_two, d_upward, activated, gathered, att_part, branch_all)
    first = lax.psum_scatter(first, ("x", "c"), scatter_dimension=0, tiled=True)
    d_kv = total(swap(d_kv, "y")).astype(LOW)
    d_qkv = jnp.concatenate([d_query, d_kv], axis=1)
    d_normed = dot(d_qkv, qkv_part, ((1,), (1,)))
    d_gain_one = jnp.sum(d_normed * hat_one, axis=0)
    d_shift_one = jnp.sum(d_normed, axis=0)
    d_qkv_w = dot(normed_one, d_qkv, ((0,), (0,))).astype(LOW)

    d_qkv_sum = jnp.sum(d_qkv.astype(WIDE), axis=0)
    here = (jnp.arange(4) == iz).astype(WIDE)[:, None, None, None]
    of_z = jnp.concatenate(
        [
            d_qkv_sum[:WIDTH].reshape(4, 1, 48),
            d_qkv_sum[2 * WIDTH :].reshape(4, 1, 48),
            d_bias_up.reshape(4, 4, 48),
        ],
        axis=1,
    )
    of_all = jnp.stack(
        [
            jnp.sum(d_branch.astype(WIDE), axis=0),
            jnp.sum(cotangent.astype(WIDE), axis=0),
            d_gain_one,
            d_shift_one,
            d_gain_two,
            d_shift_two,
        ]
    )
    smalls = jnp.concatenate(
        [
            (of_z[None] * here).reshape(16, 6, 48),
            of_all.reshape(6, 16, 48).swapaxes(0, 1),
        ],
        axis=1,
    )
    smalls = jnp.pad(smalls.astype(LOW), ((0, 0), (0, 36), (0, 144)))
    second = jnp.concatenate([d_qkv_w.reshape(16, 48, 576), smalls], axis=2)
    got = other_core(lanes(second, 1 - ic))
    second = (lanes(second, ic).astype(WIDE) + got.astype(WIDE)).astype(LOW)
    second, late_normed = lax.optimization_barrier((second, d_normed))
    second = second.reshape(4, 4, 48, half).swapaxes(0, 1).reshape(4, 192, half)
    second = jnp.concatenate([first.reshape(4, TOK, half), second], axis=1)
    second = total(swap(second, "y")).astype(LOW)
    last = jnp.concatenate([late_normed.astype(LOW), out_part], axis=1).reshape(4, TOK, 2 * D)
    last = lax.psum_scatter(last, "z", scatter_dimension=0).astype(WIDE)
    d_normed = last[:, :D]
    out_tokens = (middle + last[:, D:] + bias_down).astype(LOW)
    d_tokens = (
        d_middle + norm_back(mine(hat_one), mine(inverse_one), gain_one, d_normed)
    ).astype(LOW)

    here_x = (jnp.arange(4) == ix)[:, None, None, None]
    spread = jnp.pad(second[TOK:].reshape(4, 48, half), ((0, 0), (0, 16), (0, 0)))
    joint = jnp.concatenate(
        [
            jnp.where(here_x, second[:64].reshape(1, 4, 16, half), jnp.zeros((), LOW)),
            spread.reshape(4, 4, 16, half).swapaxes(0, 1),
        ],
        axis=2,
    ).reshape(16, 32, half)
    joint = total(swap(joint, ("x", "z")).reshape(4, 4, 32, half)).astype(LOW)
    rows = second[64:TOK]
    whole = share(jnp.concatenate([joint.reshape(TOK, half), rows], axis=0), "x")
    theirs = other_core(whole)
    grads = unpack(ic.astype(jnp.int32)[None], whole, theirs)
    return (out_tokens, d_tokens) + grads[:4] + tuple(item[0] for item in grads[4:])


def solution(mesh):
    parts = Mesh(mesh.devices.reshape(4, 2, 4, 4), ("x", "c", "z", "y"))
    every = ("x", "c", "z", "y")
    group = ("z", "y")
    row, line = P(group, None), P(group)
    return jax.shard_map(
        body,
        mesh=parts,
        in_specs=(P(every, None), P(every)) + (row,) * 4 + (line,) * 9 + (P(every, None),),
        out_specs=(P(every, None),) * 2 + (row,) * 4 + (line,) * 9,
        check_vma=False,
    )
```

```python
import jax
import jax.numpy as jnp
from jax import lax
from jax.experimental import pallas as pl
from jax.experimental.pallas import tpu as pltpu
from jax.sharding import Mesh, PartitionSpec as P

HD = 64
TOK = 128
D = 768
HEADS = 3
WIDTH = HEADS * HD
CHUNK = 512
LOW = jnp.bfloat16
WIDE = jnp.float32


def dot(left, right, dims=((1,), (0,))):
    return lax.dot_general(left, right, (dims, ((), ())), preferred_element_type=WIDE)


def masked(scores, start, place, chunk, block):
    if chunk != block and chunk != 0 and block != 3:
        return scores
    spots = lax.broadcasted_iota(jnp.int32, scores.shape, 0) + chunk * CHUNK
    allowed = None
    if chunk == 0 or block == 3:
        allowed = spots >= start
    if chunk == block:
        causal = spots <= place
        allowed = causal if allowed is None else allowed & causal
    return jnp.where(allowed, scores, -1e30)


def chunk_rows(kv_ref, chunk, low, high):
    return jnp.concatenate(
        [kv_ref[y, chunk * TOK : (chunk + 1) * TOK, low:high] for y in range(4)], axis=0
    )


def forward_kernel(q_ref, kv_ref, bound_ref, att_ref, lse_ref):
    for block in range(4):
        rows = slice(block * TOK, (block + 1) * TOK)
        start = bound_ref[0:1, rows]
        place = bound_ref[1:2, rows]
        for head in range(HEADS):
            cols = slice(head * HD, (head + 1) * HD)
            query = q_ref[rows, cols]
            scores = []
            for chunk in range(block + 1):
                keys = chunk_rows(kv_ref, chunk, head * HD, head * HD + HD)
                scores.append(
                    masked(dot(keys, query, ((1,), (1,))), start, place, chunk, block)
                )
            top = scores[0].max(axis=0, keepdims=True)
            for item in scores[1:]:
                top = jnp.maximum(top, item.max(axis=0, keepdims=True))
            total = jnp.zeros((1, TOK), WIDE)
            summed = jnp.zeros((HD, TOK), WIDE)
            for chunk in range(block + 1):
                weights = jnp.exp(scores[chunk] - top)
                total = total + weights.sum(axis=0, keepdims=True)
                values = chunk_rows(kv_ref, chunk, WIDTH + head * HD, WIDTH + head * HD + HD)
                summed = summed + dot(values, weights.astype(LOW), ((0,), (0,)))
            att_ref[rows, cols] = jnp.transpose(summed / total).astype(LOW)
            lse_ref[head : head + 1, rows] = top + jnp.log(total)


def backward_kernel(q_ref, kv_ref, bound_ref, lse_ref, do_ref, dq_ref, dkv_ref, p_ref, ds_ref):
    for head in range(HEADS):
        cols = slice(head * HD, (head + 1) * HD)
        for block in range(4):
            rows = slice(block * TOK, (block + 1) * TOK)
            start = bound_ref[0:1, rows]
            place = bound_ref[1:2, rows]
            query = q_ref[rows, cols]
            d_out = do_ref[rows, cols]
            lse = lse_ref[head : head + 1, rows]
            delta = jnp.zeros((1, TOK), WIDE)
            probs, d_probs = [], []
            for chunk in range(block + 1):
                keys = chunk_rows(kv_ref, chunk, head * HD, head * HD + HD)
                scores = masked(dot(keys, query, ((1,), (1,))), start, place, chunk, block)
                prob = jnp.exp(scores - lse)
                values = chunk_rows(kv_ref, chunk, WIDTH + head * HD, WIDTH + head * HD + HD)
                d_prob = dot(values, d_out, ((1,), (1,)))
                delta = delta + (prob * d_prob).sum(axis=0, keepdims=True)
                p_ref[chunk * CHUNK : (chunk + 1) * CHUNK, rows] = prob.astype(LOW)
                probs.append(prob)
                d_probs.append(d_prob)
            d_query = jnp.zeros((HD, TOK), WIDE)
            for chunk in range(block + 1):
                d_score = (probs[chunk] * (d_probs[chunk] - delta)).astype(LOW)
                ds_ref[chunk * CHUNK : (chunk + 1) * CHUNK, rows] = d_score
                keys = chunk_rows(kv_ref, chunk, head * HD, head * HD + HD)
                d_query = d_query + dot(keys, d_score, ((0,), (0,)))
            dq_ref[rows, cols] = (jnp.transpose(d_query) * (HD**-0.5)).astype(LOW)
        for chunk in range(4):
            spots = slice(chunk * CHUNK, (chunk + 1) * CHUNK)
            later = slice(chunk * TOK, 4 * TOK)
            d_keys = dot(ds_ref[spots, later], q_ref[later, cols]).astype(LOW)
            d_values = dot(p_ref[spots, later], do_ref[later, cols]).astype(LOW)
            for y in range(4):
                part = slice(y * TOK, (y + 1) * TOK)
                place_rows = slice(chunk * TOK, (chunk + 1) * TOK)
                dkv_ref[y, place_rows, cols] = d_keys[part]
                dkv_ref[y, place_rows, WIDTH + head * HD : WIDTH + head * HD + HD] = d_values[part]


def ffn_kernel(
    own_ref,
    early_ref,
    att_ref,
    gathered_ref,
    up_ref,
    plain_ref,
    wide_ref,
    bias_ref,
    middle_ref,
    normed_hbm,
    act_hbm,
    d_up_hbm,
    d_normed_ref,
    out_hbm,
    sums_ref,
    mid_scr,
    up_scr,
    down_scr,
    cot_scr,
    normed_ref,
    act_ref,
    d_up_ref,
    out_ref,
    sems,
):
    copies = [
        pltpu.make_async_copy(source, target, sems.at[index])
        for index, (source, target) in enumerate(
            (
                (normed_ref, normed_hbm),
                (act_ref, act_hbm),
                (d_up_ref, d_up_hbm),
                (out_ref, out_hbm),
            )
        )
    ]
    for z in range(4):
        for y in range(4):
            row = (4 * z + y) * 48
            up_scr[row : row + 48] = up_ref[y, 48 * z : 48 * z + 48]
        down_scr[192 * z : 192 * z + 192] = plain_ref[z, 0:192]
        cot_scr[TOK * z : TOK * z + TOK] = gathered_ref[z, 0:TOK]
        mid_scr[TOK * z : TOK * z + TOK] = early_ref[z, 0:TOK].astype(WIDE)
    middle = mid_scr[...] + wide_ref[2:3, :]
    for z in range(4):
        middle = middle + dot(att_ref[z], gathered_ref[z, TOK : TOK + 192])
    mid_scr[...] = middle
    middle_ref[...] = mid_scr[pl.ds(pl.multiple_of(own_ref[0] * TOK, TOK), TOK), :]
    average = jnp.mean(middle, axis=-1, keepdims=True)
    centered = middle - average
    variance = jnp.mean(centered * centered, axis=-1, keepdims=True)
    hat = centered * lax.rsqrt(variance + 1e-05)
    normed = (hat * wide_ref[6:7, :] + wide_ref[7:8, :]).astype(LOW)
    normed_ref[...] = normed
    copies[0].start()
    upward = dot(normed, up_scr[...]) + bias_ref[...]
    root = 0.7978845608028654
    square = upward * upward
    bend = jnp.tanh(root * (upward + 0.044715 * (square * upward)))
    level = 0.5 * (1.0 + bend)
    activated = (upward * level).astype(LOW)
    act_ref[...] = activated
    copies[1].start()
    out_ref[...] = dot(activated, down_scr[...]).astype(LOW)
    copies[3].start()
    slope = level + 0.5 * upward * (1.0 - bend * bend) * (root * (1.0 + 0.134145 * square))
    d_act = dot(cot_scr[...], down_scr[...], ((1,), (1,)))
    d_upward = (d_act * slope).astype(LOW)
    d_up_ref[...] = d_upward
    copies[2].start()
    d_normed = dot(d_upward, up_scr[...], ((1,), (1,)))
    d_normed_ref[...] = d_normed.astype(LOW)
    sums_ref[0:1, :] = jnp.sum(d_normed * hat, axis=0, keepdims=True)
    sums_ref[1:2, :] = jnp.sum(d_normed, axis=0, keepdims=True)
    sums_ref[2:3, :] = jnp.sum(d_upward.astype(WIDE), axis=0, keepdims=True)
    sums_ref[3:8, :] = jnp.zeros((5, D), WIDE)
    for copy in copies:
        copy.wait()


def grad_kernel(normed_ref, d_up_ref, act_ref, gathered_ref, att_ref, branch_ref, out_ref, cot_scr):
    half = D // 2
    for z in range(4):
        cot_scr[TOK * z : TOK * z + TOK] = gathered_ref[z, 0:TOK]
    up = dot(normed_ref[...], d_up_ref[...], ((0,), (0,))).astype(LOW)
    down = dot(act_ref[...], cot_scr[...], ((0,), (0,))).astype(LOW)
    proj = dot(att_ref[...], branch_ref[...], ((0,), (0,))).astype(LOW)
    blank = jnp.zeros((16, half), LOW)
    for x in range(4):
        for core in range(2):
            cols = slice(core * half, core * half + half)
            slot = 2 * x + core
            for y in range(4):
                base = TOK * y
                for z in range(4):
                    row = (4 * z + y) * 48 + 16 * x
                    out_ref[slot, base + 16 * z : base + 16 * z + 16] = (
                        up[row : row + 16, cols] if x < 3 else blank
                    )
                row = 192 * y + 48 * x
                out_ref[slot, base + 64 : base + 112] = down[row : row + 48, cols]
                row = 48 * y + 16 * x
                out_ref[slot, base + 112 : base + 128] = (
                    proj[row : row + 16, cols] if x < 3 else blank
                )


def tail_kernel(
    own_ref,
    moved_ref,
    query_ref,
    weight_ref,
    normed_ref,
    early_ref,
    sums_ref,
    branch_ref,
    cot_ref,
    d_normed_ref,
    out_ref,
    hat_scr,
):
    half = D // 2
    for z in range(4):
        hat_scr[TOK * z : TOK * z + TOK] = early_ref[z, 0:TOK].astype(WIDE)
    inputs = hat_scr[...]
    centered = inputs - jnp.mean(inputs, axis=-1, keepdims=True)
    variance = jnp.mean(centered * centered, axis=-1, keepdims=True)
    hat = centered * lax.rsqrt(variance + 1e-05)
    d_kv = moved_ref[0].astype(WIDE)
    for y in range(1, 4):
        d_kv = d_kv + moved_ref[y].astype(WIDE)
    d_qkv = jnp.concatenate([query_ref[...].astype(WIDE), d_kv], axis=1).astype(LOW)
    d_normed = dot(d_qkv, weight_ref[...], ((1,), (1,)))
    d_normed_ref[...] = d_normed.astype(LOW)
    d_weight = dot(normed_ref[...], d_qkv, ((0,), (0,)))
    columns = jnp.sum(d_qkv.astype(WIDE), axis=0, keepdims=True)
    wide_rows = [
        jnp.sum(branch_ref[...].astype(WIDE), axis=0, keepdims=True),
        jnp.sum(cot_ref[...].astype(WIDE), axis=0, keepdims=True),
        jnp.sum(d_normed * hat, axis=0, keepdims=True),
        jnp.sum(d_normed, axis=0, keepdims=True),
        sums_ref[0:1, :],
        sums_ref[1:2, :],
    ]
    hidden = sums_ref[2:3, :]
    for y in range(4):
        low = 48 * y
        own_rows = [
            columns[:, low : low + 48],
            columns[:, 2 * WIDTH + low : 2 * WIDTH + low + 48],
        ] + [hidden[:, 192 * y + 48 * i : 192 * y + 48 * i + 48] for i in range(4)]
        own_rows = jnp.concatenate(own_rows, axis=0)
        for z in range(4):
            low = 48 * (4 * z + y)
            short = jnp.concatenate(
                [jnp.where(own_ref[0] == z, own_rows, 0.0)]
                + [item[:, low : low + 48] for item in wide_rows]
                + [jnp.zeros((36, 48), WIDE)],
                axis=0,
            )
            block = d_weight[low : low + 48]
            out_ref[0, y, 48 * z : 48 * z + 48] = block[:, :half].astype(LOW)
            out_ref[1, y, 48 * z : 48 * z + 48] = jnp.concatenate(
                [block[:, half:], short, jnp.zeros((48, 144), WIDE)], axis=1
            ).astype(LOW)


def pack_kernel(
    tokens_hbm,
    qkv_hbm,
    up_hbm,
    down_hbm,
    proj_hbm,
    short_ref,
    hidden_ref,
    seg_ref,
    out_ref,
    plain_ref,
    tokens_ref,
    qkv_ref,
    up_ref,
    sems,
):
    pairs = (
        (tokens_hbm, tokens_ref),
        (qkv_hbm, qkv_ref),
        (up_hbm, up_ref),
        (down_hbm, plain_ref.at[pl.ds(0, 192)]),
        (proj_hbm, plain_ref.at[pl.ds(192, 48)]),
    )
    copies = [
        pltpu.make_async_copy(source, target, sems.at[index])
        for index, (source, target) in enumerate(pairs)
    ]
    for copy in copies:
        copy.start()
    seg = seg_ref[...]
    count_one = jnp.sum((seg <= 0).astype(WIDE), axis=1, keepdims=True)
    count_two = jnp.sum((seg <= 1).astype(WIDE), axis=1, keepdims=True)
    spot = lax.broadcasted_iota(jnp.int32, (1, 192), 1)
    counts = jnp.where(spot == 0, count_one, jnp.where(spot == 1, count_two, 0.0))
    side = jnp.concatenate(
        [
            jnp.concatenate(
                [short_ref[...].astype(WIDE), jnp.zeros((8, 144), WIDE)], axis=1
            ),
            jnp.concatenate(
                [hidden_ref[...].astype(WIDE), jnp.zeros((4, 144), WIDE)], axis=1
            ),
            counts,
            jnp.concatenate([seg.astype(WIDE), jnp.zeros((1, 64), WIDE)], axis=1),
            jnp.zeros((34, 192), WIDE),
        ],
        axis=0,
    ).astype(LOW)
    for copy in copies:
        copy.wait()
    for part in range(4):
        out_ref[part, 0:TOK, :] = tokens_ref[...]
        for kind in range(3):
            out_ref[part, TOK : TOK + 48, kind * WIDTH : (kind + 1) * WIDTH] = qkv_ref[
                :, kind * D + part * WIDTH : kind * D + (part + 1) * WIDTH
            ]
        out_ref[part, TOK : TOK + 48, 3 * WIDTH : D] = side
        out_ref[part, TOK + 48 : TOK + 96, :] = up_ref[:, part * D : (part + 1) * D]


def unpack_kernel(core_ref, mine_ref, theirs_ref, qkv_ref, out_ref, up_ref, down_ref, *line_refs):
    first = core_ref[0] == 0
    half = D // 2
    short = jnp.zeros((12, 48), WIDE)
    for part in range(4):
        mine = mine_ref[part].astype(WIDE)
        theirs = theirs_ref[part].astype(WIDE)
        sides = (jnp.where(first, mine, theirs), jnp.where(first, theirs, mine))
        rows = slice(16 * part, 16 * part + 16)
        for core in range(2):
            side = sides[core]
            cols = slice(core * half, (core + 1) * half)
            down_ref[part * 48 : (part + 1) * 48, cols] = side[TOK : TOK + 48]
            if part == 3:
                continue
            out_ref[rows, cols] = side[TOK + 48 : TOK + 64]
            for quarter in range(4):
                low = quarter * D + core * half
                up_ref[rows, low : low + half] = side[32 * quarter : 32 * quarter + 16]
                block = side[32 * quarter + 16 : 32 * quarter + 32]
                low = quarter * WIDTH
                if core == 0:
                    qkv_ref[rows, low : low + WIDTH] = block[:, :WIDTH]
                    qkv_ref[rows, D + low : D + low + WIDTH] = block[:, WIDTH:]
                else:
                    qkv_ref[rows, 2 * D + low : 2 * D + low + WIDTH] = block[:, :WIDTH]
                    if part == 0:
                        short = short + block[:12, WIDTH : WIDTH + 48]
    hidden = jnp.concatenate([short[2 + i : 3 + i] for i in range(4)], axis=1)
    lines = [short[i : i + 1] for i in (0, 1, 6)] + [hidden]
    lines += [short[i : i + 1] for i in range(7, 12)]
    for ref, value in zip(line_refs, lines):
        ref[...] = value


VMEM = pl.BlockSpec(memory_space=pltpu.VMEM)
FAR = pl.BlockSpec(memory_space=pltpu.HBM)
PARAMS = pltpu.CompilerParams(vmem_limit_bytes=48 * 1024 * 1024)
WHOLE = pltpu.CompilerParams(vmem_limit_bytes=60 * 1024 * 1024)


def attend_forward(query, kv, bounds):
    return pl.pallas_call(
        forward_kernel,
        out_shape=(
            jax.ShapeDtypeStruct((4 * TOK, WIDTH), LOW),
            jax.ShapeDtypeStruct((8, 4 * TOK), WIDE),
        ),
        in_specs=[VMEM] * 3,
        out_specs=(VMEM, VMEM),
        compiler_params=PARAMS,
        cost_estimate=pl.CostEstimate(
            flops=1_000_000_000, bytes_accessed=4_000_000, transcendentals=2_000_000
        ),
    )(query, kv, bounds)


def attend_backward(query, kv, bounds, lse, d_out):
    return pl.pallas_call(
        backward_kernel,
        out_shape=(
            jax.ShapeDtypeStruct((4 * TOK, WIDTH), LOW),
            jax.ShapeDtypeStruct((4, 4 * TOK, 2 * WIDTH), LOW),
        ),
        in_specs=[VMEM] * 5,
        out_specs=(VMEM, VMEM),
        scratch_shapes=[
            pltpu.VMEM((4 * CHUNK, 4 * TOK), LOW),
            pltpu.VMEM((4 * CHUNK, 4 * TOK), LOW),
        ],
        compiler_params=PARAMS,
        cost_estimate=pl.CostEstimate(
            flops=2_500_000_000, bytes_accessed=6_000_000, transcendentals=2_000_000
        ),
    )(query, kv, bounds, lse, d_out)


def feed_forward(*parts):
    return pl.pallas_call(
        ffn_kernel,
        out_shape=(
            jax.ShapeDtypeStruct((TOK, D), WIDE),
            jax.ShapeDtypeStruct((4 * TOK, D), LOW),
            jax.ShapeDtypeStruct((4 * TOK, D), LOW),
            jax.ShapeDtypeStruct((4 * TOK, D), LOW),
            jax.ShapeDtypeStruct((4 * TOK, D), LOW),
            jax.ShapeDtypeStruct((4 * TOK, D), LOW),
            jax.ShapeDtypeStruct((8, D), WIDE),
        ),
        in_specs=[pl.BlockSpec(memory_space=pltpu.SMEM)] + [VMEM] * 7,
        out_specs=(VMEM, FAR, FAR, FAR, VMEM, FAR, VMEM),
        scratch_shapes=[
            pltpu.VMEM((4 * TOK, D), WIDE),
            pltpu.VMEM((D, D), LOW),
            pltpu.VMEM((D, D), LOW),
            pltpu.VMEM((4 * TOK, D), LOW),
            pltpu.VMEM((4 * TOK, D), LOW),
            pltpu.VMEM((4 * TOK, D), LOW),
            pltpu.VMEM((4 * TOK, D), LOW),
            pltpu.VMEM((4 * TOK, D), LOW),
            pltpu.SemaphoreType.DMA((4,)),
        ],
        compiler_params=WHOLE,
        cost_estimate=pl.CostEstimate(
            flops=4_000_000_000, bytes_accessed=12_000_000, transcendentals=400_000
        ),
    )(*parts)


def weight_grads(*parts):
    return pl.pallas_call(
        grad_kernel,
        out_shape=jax.ShapeDtypeStruct((8, 4 * TOK, D // 2), LOW),
        in_specs=[VMEM] * 6,
        out_specs=VMEM,
        scratch_shapes=[pltpu.VMEM((4 * TOK, D), LOW)],
        compiler_params=PARAMS,
        cost_estimate=pl.CostEstimate(
            flops=1_400_000_000, bytes_accessed=9_000_000, transcendentals=0
        ),
    )(*parts)


def tail(*parts):
    return pl.pallas_call(
        tail_kernel,
        out_shape=(
            jax.ShapeDtypeStruct((4 * TOK, D), LOW),
            jax.ShapeDtypeStruct((2, 4, 192, D // 2), LOW),
        ),
        in_specs=[pl.BlockSpec(memory_space=pltpu.SMEM)] + [VMEM] * 8,
        out_specs=(VMEM, VMEM),
        scratch_shapes=[pltpu.VMEM((4 * TOK, D), WIDE)],
        compiler_params=PARAMS,
        cost_estimate=pl.CostEstimate(
            flops=1_000_000_000, bytes_accessed=7_000_000, transcendentals=0
        ),
    )(*parts)


def pack(*parts):
    return pl.pallas_call(
        pack_kernel,
        out_shape=(
            jax.ShapeDtypeStruct((4, TOK + 96, D), LOW),
            jax.ShapeDtypeStruct((240, D), LOW),
        ),
        in_specs=[FAR] * 5 + [VMEM] * 3,
        out_specs=(VMEM, VMEM),
        scratch_shapes=[
            pltpu.VMEM((TOK, D), LOW),
            pltpu.VMEM((48, 3 * D), LOW),
            pltpu.VMEM((48, 4 * D), LOW),
            pltpu.SemaphoreType.DMA((5,)),
        ],
        compiler_params=WHOLE,
        cost_estimate=pl.CostEstimate(
            flops=1_000_000, bytes_accessed=2_500_000, transcendentals=0
        ),
    )(*parts)


def unpack(core, mine, theirs):
    return pl.pallas_call(
        unpack_kernel,
        out_shape=tuple(
            jax.ShapeDtypeStruct(shape, WIDE)
            for shape in ((48, 3 * D), (48, D), (48, 4 * D), (192, D))
            + ((1, 48),) * 3
            + ((1, 192),)
            + ((1, 48),) * 5
        ),
        in_specs=[pl.BlockSpec(memory_space=pltpu.SMEM), VMEM, VMEM],
        out_specs=(VMEM,) * 13,
        compiler_params=PARAMS,
        cost_estimate=pl.CostEstimate(
            flops=1_000_000, bytes_accessed=3_500_000, transcendentals=0
        ),
    )(core, mine, theirs)


def norm_parts(values):
    average = jnp.mean(values, axis=-1, keepdims=True)
    centered = values - average
    variance = jnp.mean(centered * centered, axis=-1, keepdims=True)
    inverse = lax.rsqrt(variance + 1e-05)
    return centered * inverse, inverse


def norm_back(hat, inverse, gain, grad):
    scaled = grad * gain
    mean_one = jnp.mean(scaled, axis=-1, keepdims=True)
    mean_two = jnp.mean(scaled * hat, axis=-1, keepdims=True)
    return inverse * (scaled - mean_one - hat * mean_two)


def swap(value, axis):
    return lax.all_to_all(value, axis, 0, 0, tiled=True)


def share(value, axis):
    return swap(jnp.broadcast_to(value[None], (4,) + value.shape), axis)


def total(value):
    return jnp.sum(value.astype(WIDE), axis=0)


def other_core(value):
    return lax.ppermute(value, "c", [(0, 1), (1, 0)])


def body(
    tokens,
    segments,
    w_qkv,
    w_out,
    w_up,
    w_down,
    b_query,
    b_value,
    b_out,
    b_up,
    b_down,
    ln1_gain,
    ln1_shift,
    ln2_gain,
    ln2_shift,
    cotangent,
):
    ix, ic, iz, iy = (lax.axis_index(name) for name in ("x", "c", "z", "y"))
    first_doc = 3 * (2 * ix + ic)
    half = D // 2

    def lanes(value, core):
        return lax.dynamic_slice_in_dim(value, core * half, half, value.ndim - 1)

    short = jnp.stack(
        [b_query, b_value, b_out, b_down, ln1_gain, ln1_shift, ln2_gain, ln2_shift]
    )
    early, plain = pack(
        tokens,
        w_qkv,
        w_up,
        w_down,
        w_out,
        short,
        b_up.reshape(4, 48),
        (segments - first_doc)[None],
    )
    early = swap(early, "z")
    token_all = early[:, :TOK].reshape(4 * TOK, D)
    seg_all = early[:, TOK + 13, 576:704].astype(jnp.int32)
    payload = early[:, TOK : TOK + 48, :640]
    payload = jnp.broadcast_to(payload[None], (4,) + payload.shape)
    early_all = swap(payload, "y").swapaxes(0, 1)
    qkv_part = early_all[:, :, :, :576].reshape(D, 3 * WIDTH)
    small_all = early_all[:, :, :16, 576:624].astype(WIDE)
    total_counts = jnp.sum(small_all[:, :, 12, :2], axis=(0, 1)).astype(jnp.int32)
    wide = small_all.reshape(16, 16, 48)[:, :8].swapaxes(0, 1).reshape(8, D)
    bias_out, bias_down, gain_one, shift_one, gain_two, shift_two = (
        wide[index] for index in range(2, 8)
    )
    own = lax.dynamic_index_in_dim(small_all, iz, 0, keepdims=False)
    bias_query = own[:, 0].reshape(WIDTH)
    bias_value = own[:, 1].reshape(WIDTH)
    bias_up = own[:, 8:12].reshape(D)

    plain = lax.all_gather(plain, "y")
    plain, _ = lax.optimization_barrier((plain, payload))
    gathered = lax.all_gather(
        jnp.concatenate([cotangent, plain[:, 192:].reshape(192, D)], axis=0), "z"
    )
    up_rows, gathered = lax.optimization_barrier((early[:, TOK + 48 :], gathered))
    up_part = lax.all_gather(up_rows.reshape(192, D), "y")
    out_rows = lax.dynamic_index_in_dim(gathered, iz, 0, keepdims=False)[TOK:]
    cot_all = gathered[:, :TOK].reshape(4 * TOK, D)

    inputs = token_all.astype(WIDE)
    start = jnp.where(
        seg_all <= 0, 0, jnp.where(seg_all <= 1, total_counts[0], total_counts[1])
    )
    place = (
        4 * TOK * jnp.arange(4, dtype=jnp.int32)[:, None]
        + TOK * iy
        + jnp.arange(TOK, dtype=jnp.int32)[None, :]
    )
    bounds = jnp.concatenate(
        [start.reshape(1, 4 * TOK), place.reshape(1, 4 * TOK), jnp.zeros((6, 4 * TOK), jnp.int32)]
    )

    hat_one, inverse_one = norm_parts(inputs)
    normed_one = (hat_one * gain_one + shift_one).astype(LOW)
    qkv = dot(normed_one, qkv_part)
    query = ((qkv[:, :WIDTH] + bias_query).astype(LOW) * (HD**-0.5)).astype(LOW)
    kv = jnp.concatenate(
        [qkv[:, WIDTH : 2 * WIDTH], qkv[:, 2 * WIDTH :] + bias_value], axis=1
    ).astype(LOW)
    kv_all = share(kv, "y")
    att_part, lse = attend_forward(query, kv_all, bounds)
    att_all = share(att_part, "z")

    middle, normed_two, activated, d_upward, d_normed, out_part, sums = feed_forward(
        iz.astype(jnp.int32)[None], early, att_all, gathered, up_part, plain, wide, bias_up[None]
    )
    d_normed = total(swap(d_normed.reshape(4, TOK, D), "z"))
    own_rows = iz * TOK

    def mine(value):
        return lax.dynamic_slice_in_dim(value, own_rows, TOK, 0)

    hat_two, inverse_two = norm_parts(middle)
    d_middle = cotangent.astype(WIDE) + norm_back(hat_two, inverse_two, gain_two, d_normed)
    d_branch = d_middle.astype(LOW)
    branch_all = share(d_branch, "z").reshape(4 * TOK, D)
    d_attended = dot(branch_all, out_rows, ((1,), (1,))).astype(LOW)

    d_query, d_kv = attend_backward(query, kv_all, bounds, lse, d_attended)

    first = weight_grads(normed_two, d_upward, activated, gathered, att_part, branch_all)
    first = lax.psum_scatter(first, ("x", "c"), scatter_dimension=0, tiled=True)
    d_kv = swap(d_kv, "y")
    d_normed, second = tail(
        iz.astype(jnp.int32)[None],
        d_kv,
        d_query,
        qkv_part,
        normed_one,
        early,
        sums,
        d_branch,
        cotangent,
    )
    got = other_core(lax.dynamic_index_in_dim(second, 1 - ic, 0, keepdims=False))
    second = lax.dynamic_index_in_dim(second, ic, 0, keepdims=False)
    second = (second.astype(WIDE) + got.astype(WIDE)).astype(LOW)
    second, late_normed = lax.optimization_barrier((second, d_normed))
    second = jnp.concatenate([first.reshape(4, TOK, half), second], axis=1)
    second = total(swap(second, "y")).astype(LOW)
    last = jnp.concatenate([late_normed, out_part], axis=1).reshape(4, TOK, 2 * D)
    last = lax.psum_scatter(last, "z", scatter_dimension=0).astype(WIDE)
    d_normed = last[:, :D]
    out_tokens = (middle + last[:, D:] + bias_down).astype(LOW)
    d_tokens = (
        d_middle + norm_back(mine(hat_one), mine(inverse_one), gain_one, d_normed)
    ).astype(LOW)

    here_x = (jnp.arange(4) == ix)[:, None, None, None]
    spread = jnp.pad(second[TOK:].reshape(4, 48, half), ((0, 0), (0, 16), (0, 0)))
    joint = jnp.concatenate(
        [
            jnp.where(here_x, second[:64].reshape(1, 4, 16, half), jnp.zeros((), LOW)),
            spread.reshape(4, 4, 16, half).swapaxes(0, 1),
        ],
        axis=2,
    ).reshape(16, 32, half)
    joint = total(swap(joint, ("x", "z")).reshape(4, 4, 32, half)).astype(LOW)
    rows = second[64:TOK]
    whole = share(jnp.concatenate([joint.reshape(TOK, half), rows], axis=0), "x")
    theirs = other_core(whole)
    grads = unpack(ic.astype(jnp.int32)[None], whole, theirs)
    return (out_tokens, d_tokens) + grads[:4] + tuple(item[0] for item in grads[4:])


def solution(mesh):
    parts = Mesh(mesh.devices.reshape(4, 2, 4, 4), ("x", "c", "z", "y"))
    every = ("x", "c", "z", "y")
    group = ("z", "y")
    row, line = P(group, None), P(group)
    return jax.shard_map(
        body,
        mesh=parts,
        in_specs=(P(every, None), P(every)) + (row,) * 4 + (line,) * 9 + (P(every, None),),
        out_specs=(P(every, None),) * 2 + (row,) * 4 + (line,) * 9,
        check_vma=False,
    )
```

```python
import jax
import jax.numpy as jnp
from jax import lax
from jax.experimental import pallas as pl
from jax.experimental.pallas import tpu as pltpu
from jax.sharding import Mesh, PartitionSpec as P

HD = 64
TOK = 128
D = 768
HEADS = 3
WIDTH = HEADS * HD
CHUNK = 512
LOW = jnp.bfloat16
WIDE = jnp.float32


def dot(left, right, dims=((1,), (0,))):
    return lax.dot_general(left, right, (dims, ((), ())), preferred_element_type=WIDE)


def masked(scores, start, place, chunk, block):
    if chunk != block and chunk != 0 and block != 3:
        return scores
    spots = lax.broadcasted_iota(jnp.int32, scores.shape, 0) + chunk * CHUNK
    allowed = None
    if chunk == 0 or block == 3:
        allowed = spots >= start
    if chunk == block:
        causal = spots <= place
        allowed = causal if allowed is None else allowed & causal
    return jnp.where(allowed, scores, -1e30)


def chunk_rows(kv_ref, chunk, low, high):
    return jnp.concatenate(
        [kv_ref[y, chunk * TOK : (chunk + 1) * TOK, low:high] for y in range(4)], axis=0
    )


def forward_kernel(q_ref, kv_ref, bound_ref, att_ref, lse_ref):
    for block in range(4):
        rows = slice(block * TOK, (block + 1) * TOK)
        start = bound_ref[0:1, rows]
        place = bound_ref[1:2, rows]
        for head in range(HEADS):
            cols = slice(head * HD, (head + 1) * HD)
            query = q_ref[rows, cols]
            scores = []
            for chunk in range(block + 1):
                keys = chunk_rows(kv_ref, chunk, head * HD, head * HD + HD)
                scores.append(
                    masked(dot(keys, query, ((1,), (1,))), start, place, chunk, block)
                )
            top = scores[0].max(axis=0, keepdims=True)
            for item in scores[1:]:
                top = jnp.maximum(top, item.max(axis=0, keepdims=True))
            total = jnp.zeros((1, TOK), WIDE)
            summed = jnp.zeros((HD, TOK), WIDE)
            for chunk in range(block + 1):
                weights = jnp.exp(scores[chunk] - top)
                total = total + weights.sum(axis=0, keepdims=True)
                values = chunk_rows(kv_ref, chunk, WIDTH + head * HD, WIDTH + head * HD + HD)
                summed = summed + dot(values, weights.astype(LOW), ((0,), (0,)))
            mixed = jnp.transpose(summed / total).astype(LOW)
            for copy in range(4):
                att_ref[copy, rows, cols] = mixed
            lse_ref[head : head + 1, rows] = top + jnp.log(total)


def backward_kernel(q_ref, kv_ref, bound_ref, lse_ref, do_ref, dq_ref, dkv_ref, p_ref, ds_ref):
    for head in range(HEADS):
        cols = slice(head * HD, (head + 1) * HD)
        for block in range(4):
            rows = slice(block * TOK, (block + 1) * TOK)
            start = bound_ref[0:1, rows]
            place = bound_ref[1:2, rows]
            query = q_ref[rows, cols]
            d_out = do_ref[rows, cols]
            lse = lse_ref[head : head + 1, rows]
            delta = jnp.zeros((1, TOK), WIDE)
            probs, d_probs = [], []
            for chunk in range(block + 1):
                keys = chunk_rows(kv_ref, chunk, head * HD, head * HD + HD)
                scores = masked(dot(keys, query, ((1,), (1,))), start, place, chunk, block)
                prob = jnp.exp(scores - lse)
                values = chunk_rows(kv_ref, chunk, WIDTH + head * HD, WIDTH + head * HD + HD)
                d_prob = dot(values, d_out, ((1,), (1,)))
                delta = delta + (prob * d_prob).sum(axis=0, keepdims=True)
                p_ref[chunk * CHUNK : (chunk + 1) * CHUNK, rows] = prob.astype(LOW)
                probs.append(prob)
                d_probs.append(d_prob)
            d_query = jnp.zeros((HD, TOK), WIDE)
            for chunk in range(block + 1):
                d_score = (probs[chunk] * (d_probs[chunk] - delta)).astype(LOW)
                ds_ref[chunk * CHUNK : (chunk + 1) * CHUNK, rows] = d_score
                keys = chunk_rows(kv_ref, chunk, head * HD, head * HD + HD)
                d_query = d_query + dot(keys, d_score, ((0,), (0,)))
            dq_ref[rows, cols] = (jnp.transpose(d_query) * (HD**-0.5)).astype(LOW)
        for chunk in range(4):
            spots = slice(chunk * CHUNK, (chunk + 1) * CHUNK)
            later = slice(chunk * TOK, 4 * TOK)
            d_keys = dot(ds_ref[spots, later], q_ref[later, cols]).astype(LOW)
            d_values = dot(p_ref[spots, later], do_ref[later, cols]).astype(LOW)
            for y in range(4):
                part = slice(y * TOK, (y + 1) * TOK)
                place_rows = slice(chunk * TOK, (chunk + 1) * TOK)
                dkv_ref[y, place_rows, cols] = d_keys[part]
                dkv_ref[y, place_rows, WIDTH + head * HD : WIDTH + head * HD + HD] = d_values[part]


def ffn_kernel(
    own_ref,
    early_ref,
    att_ref,
    gathered_ref,
    up_ref,
    plain_ref,
    wide_ref,
    bias_ref,
    middle_ref,
    normed_hbm,
    act_hbm,
    d_up_hbm,
    d_normed_ref,
    out_hbm,
    sums_ref,
    mid_scr,
    up_scr,
    down_scr,
    cot_scr,
    normed_ref,
    act_ref,
    d_up_ref,
    out_ref,
    sems,
):
    copies = [
        pltpu.make_async_copy(source, target, sems.at[index])
        for index, (source, target) in enumerate(
            (
                (normed_ref, normed_hbm),
                (act_ref, act_hbm),
                (d_up_ref, d_up_hbm),
                (out_ref, out_hbm),
            )
        )
    ]
    for z in range(4):
        for y in range(4):
            row = (4 * z + y) * 48
            up_scr[row : row + 48] = up_ref[y, 48 * z : 48 * z + 48]
        down_scr[192 * z : 192 * z + 192] = plain_ref[z, 0:192]
        cot_scr[TOK * z : TOK * z + TOK] = gathered_ref[z, 0:TOK]
        mid_scr[TOK * z : TOK * z + TOK] = early_ref[z, 0:TOK].astype(WIDE)
    middle = mid_scr[...] + wide_ref[2:3, :]
    for z in range(4):
        middle = middle + dot(att_ref[z], gathered_ref[z, TOK : TOK + 192])
    mid_scr[...] = middle
    middle_ref[...] = mid_scr[pl.ds(pl.multiple_of(own_ref[0] * TOK, TOK), TOK), :]
    average = jnp.mean(middle, axis=-1, keepdims=True)
    centered = middle - average
    variance = jnp.mean(centered * centered, axis=-1, keepdims=True)
    hat = centered * lax.rsqrt(variance + 1e-05)
    normed = (hat * wide_ref[6:7, :] + wide_ref[7:8, :]).astype(LOW)
    normed_ref[...] = normed
    copies[0].start()
    upward = dot(normed, up_scr[...]) + bias_ref[...]
    root = 0.7978845608028654
    square = upward * upward
    bend = jnp.tanh(root * (upward + 0.044715 * (square * upward)))
    level = 0.5 * (1.0 + bend)
    activated = (upward * level).astype(LOW)
    act_ref[...] = activated
    copies[1].start()
    out_ref[...] = dot(activated, down_scr[...]).astype(LOW)
    copies[3].start()
    slope = level + 0.5 * upward * (1.0 - bend * bend) * (root * (1.0 + 0.134145 * square))
    d_act = dot(cot_scr[...], down_scr[...], ((1,), (1,)))
    d_upward = (d_act * slope).astype(LOW)
    d_up_ref[...] = d_upward
    copies[2].start()
    d_normed = dot(d_upward, up_scr[...], ((1,), (1,)))
    d_normed_ref[...] = d_normed.astype(LOW)
    sums_ref[0:1, :] = jnp.sum(d_normed * hat, axis=0, keepdims=True)
    sums_ref[1:2, :] = jnp.sum(d_normed, axis=0, keepdims=True)
    sums_ref[2:3, :] = jnp.sum(d_upward.astype(WIDE), axis=0, keepdims=True)
    sums_ref[3:8, :] = jnp.zeros((5, D), WIDE)
    for copy in copies:
        copy.wait()


def grad_kernel(normed_ref, d_up_ref, act_ref, gathered_ref, att_ref, branch_ref, out_ref, cot_scr):
    half = D // 2
    for z in range(4):
        cot_scr[TOK * z : TOK * z + TOK] = gathered_ref[z, 0:TOK]
    up = dot(normed_ref[...], d_up_ref[...], ((0,), (0,))).astype(LOW)
    down = dot(act_ref[...], cot_scr[...], ((0,), (0,))).astype(LOW)
    proj = dot(att_ref[0], branch_ref[...], ((0,), (0,))).astype(LOW)
    blank = jnp.zeros((16, half), LOW)
    for x in range(4):
        for core in range(2):
            cols = slice(core * half, core * half + half)
            slot = 2 * x + core
            for y in range(4):
                base = TOK * y
                for z in range(4):
                    row = (4 * z + y) * 48 + 16 * x
                    out_ref[slot, base + 16 * z : base + 16 * z + 16] = (
                        up[row : row + 16, cols] if x < 3 else blank
                    )
                row = 192 * y + 48 * x
                out_ref[slot, base + 64 : base + 112] = down[row : row + 48, cols]
                row = 48 * y + 16 * x
                out_ref[slot, base + 112 : base + 128] = (
                    proj[row : row + 16, cols] if x < 3 else blank
                )


def tail_kernel(
    own_ref,
    moved_ref,
    query_ref,
    weight_ref,
    normed_ref,
    early_ref,
    sums_ref,
    branch_ref,
    cot_ref,
    d_normed_ref,
    out_ref,
    hat_scr,
):
    half = D // 2
    for z in range(4):
        hat_scr[TOK * z : TOK * z + TOK] = early_ref[z, 0:TOK].astype(WIDE)
    inputs = hat_scr[...]
    centered = inputs - jnp.mean(inputs, axis=-1, keepdims=True)
    variance = jnp.mean(centered * centered, axis=-1, keepdims=True)
    hat = centered * lax.rsqrt(variance + 1e-05)
    d_kv = moved_ref[0].astype(WIDE)
    for y in range(1, 4):
        d_kv = d_kv + moved_ref[y].astype(WIDE)
    d_qkv = jnp.concatenate([query_ref[...].astype(WIDE), d_kv], axis=1).astype(LOW)
    d_normed = dot(d_qkv, weight_ref[...], ((1,), (1,)))
    d_normed_ref[...] = d_normed.astype(LOW)
    d_weight = dot(normed_ref[...], d_qkv, ((0,), (0,)))
    columns = jnp.sum(d_qkv.astype(WIDE), axis=0, keepdims=True)
    wide_rows = [
        jnp.sum(branch_ref[...].astype(WIDE), axis=0, keepdims=True),
        jnp.sum(cot_ref[...].astype(WIDE), axis=0, keepdims=True),
        jnp.sum(d_normed * hat, axis=0, keepdims=True),
        jnp.sum(d_normed, axis=0, keepdims=True),
        sums_ref[0:1, :],
        sums_ref[1:2, :],
    ]
    hidden = sums_ref[2:3, :]
    for y in range(4):
        low = 48 * y
        own_rows = [
            columns[:, low : low + 48],
            columns[:, 2 * WIDTH + low : 2 * WIDTH + low + 48],
        ] + [hidden[:, 192 * y + 48 * i : 192 * y + 48 * i + 48] for i in range(4)]
        own_rows = jnp.concatenate(own_rows, axis=0)
        for z in range(4):
            low = 48 * (4 * z + y)
            short = jnp.concatenate(
                [jnp.where(own_ref[0] == z, own_rows, 0.0)]
                + [item[:, low : low + 48] for item in wide_rows]
                + [jnp.zeros((36, 48), WIDE)],
                axis=0,
            )
            block = d_weight[low : low + 48]
            out_ref[0, y, 48 * z : 48 * z + 48] = block[:, :half].astype(LOW)
            out_ref[1, y, 48 * z : 48 * z + 48] = jnp.concatenate(
                [block[:, half:], short, jnp.zeros((48, 144), WIDE)], axis=1
            ).astype(LOW)


def pack_kernel(
    tokens_hbm,
    qkv_hbm,
    up_hbm,
    down_hbm,
    proj_hbm,
    short_ref,
    hidden_ref,
    seg_ref,
    out_ref,
    plain_ref,
    tokens_ref,
    qkv_ref,
    up_ref,
    sems,
):
    pairs = (
        (tokens_hbm, tokens_ref),
        (qkv_hbm, qkv_ref),
        (up_hbm, up_ref),
        (down_hbm, plain_ref.at[pl.ds(0, 192)]),
        (proj_hbm, plain_ref.at[pl.ds(192, 48)]),
    )
    copies = [
        pltpu.make_async_copy(source, target, sems.at[index])
        for index, (source, target) in enumerate(pairs)
    ]
    for copy in copies:
        copy.start()
    seg = seg_ref[...]
    count_one = jnp.sum((seg <= 0).astype(WIDE), axis=1, keepdims=True)
    count_two = jnp.sum((seg <= 1).astype(WIDE), axis=1, keepdims=True)
    spot = lax.broadcasted_iota(jnp.int32, (1, 192), 1)
    counts = jnp.where(spot == 0, count_one, jnp.where(spot == 1, count_two, 0.0))
    side = jnp.concatenate(
        [
            jnp.concatenate(
                [short_ref[...].astype(WIDE), jnp.zeros((8, 144), WIDE)], axis=1
            ),
            jnp.concatenate(
                [hidden_ref[...].astype(WIDE), jnp.zeros((4, 144), WIDE)], axis=1
            ),
            counts,
            jnp.concatenate([seg.astype(WIDE), jnp.zeros((1, 64), WIDE)], axis=1),
            jnp.zeros((34, 192), WIDE),
        ],
        axis=0,
    ).astype(LOW)
    for copy in copies:
        copy.wait()
    for part in range(4):
        out_ref[part, 0:TOK, :] = tokens_ref[...]
        for kind in range(3):
            out_ref[part, TOK : TOK + 48, kind * WIDTH : (kind + 1) * WIDTH] = qkv_ref[
                :, kind * D + part * WIDTH : kind * D + (part + 1) * WIDTH
            ]
        out_ref[part, TOK : TOK + 48, 3 * WIDTH : D] = side
        out_ref[part, TOK + 48 : TOK + 96, :] = up_ref[:, part * D : (part + 1) * D]


def unpack_kernel(core_ref, mine_ref, theirs_ref, qkv_ref, out_ref, up_ref, down_ref, *line_refs):
    first = core_ref[0] == 0
    half = D // 2
    short = jnp.zeros((12, 48), WIDE)
    for part in range(4):
        mine = mine_ref[part].astype(WIDE)
        theirs = theirs_ref[part].astype(WIDE)
        sides = (jnp.where(first, mine, theirs), jnp.where(first, theirs, mine))
        rows = slice(16 * part, 16 * part + 16)
        for core in range(2):
            side = sides[core]
            cols = slice(core * half, (core + 1) * half)
            down_ref[part * 48 : (part + 1) * 48, cols] = side[TOK : TOK + 48]
            if part == 3:
                continue
            out_ref[rows, cols] = side[TOK + 48 : TOK + 64]
            for quarter in range(4):
                low = quarter * D + core * half
                up_ref[rows, low : low + half] = side[32 * quarter : 32 * quarter + 16]
                block = side[32 * quarter + 16 : 32 * quarter + 32]
                low = quarter * WIDTH
                if core == 0:
                    qkv_ref[rows, low : low + WIDTH] = block[:, :WIDTH]
                    qkv_ref[rows, D + low : D + low + WIDTH] = block[:, WIDTH:]
                else:
                    qkv_ref[rows, 2 * D + low : 2 * D + low + WIDTH] = block[:, :WIDTH]
                    if part == 0:
                        short = short + block[:12, WIDTH : WIDTH + 48]
    hidden = jnp.concatenate([short[2 + i : 3 + i] for i in range(4)], axis=1)
    lines = [short[i : i + 1] for i in (0, 1, 6)] + [hidden]
    lines += [short[i : i + 1] for i in range(7, 12)]
    for ref, value in zip(line_refs, lines):
        ref[...] = value


VMEM = pl.BlockSpec(memory_space=pltpu.VMEM)
FAR = pl.BlockSpec(memory_space=pltpu.HBM)
PARAMS = pltpu.CompilerParams(vmem_limit_bytes=48 * 1024 * 1024)
WHOLE = pltpu.CompilerParams(vmem_limit_bytes=60 * 1024 * 1024)


def attend_forward(query, kv, bounds):
    return pl.pallas_call(
        forward_kernel,
        out_shape=(
            jax.ShapeDtypeStruct((4, 4 * TOK, WIDTH), LOW),
            jax.ShapeDtypeStruct((8, 4 * TOK), WIDE),
        ),
        in_specs=[VMEM] * 3,
        out_specs=(VMEM, VMEM),
        compiler_params=PARAMS,
        cost_estimate=pl.CostEstimate(
            flops=1_000_000_000, bytes_accessed=4_000_000, transcendentals=2_000_000
        ),
    )(query, kv, bounds)


def attend_backward(query, kv, bounds, lse, d_out):
    return pl.pallas_call(
        backward_kernel,
        out_shape=(
            jax.ShapeDtypeStruct((4 * TOK, WIDTH), LOW),
            jax.ShapeDtypeStruct((4, 4 * TOK, 2 * WIDTH), LOW),
        ),
        in_specs=[VMEM] * 5,
        out_specs=(VMEM, VMEM),
        scratch_shapes=[
            pltpu.VMEM((4 * CHUNK, 4 * TOK), LOW),
            pltpu.VMEM((4 * CHUNK, 4 * TOK), LOW),
        ],
        compiler_params=PARAMS,
        cost_estimate=pl.CostEstimate(
            flops=2_500_000_000, bytes_accessed=6_000_000, transcendentals=2_000_000
        ),
    )(query, kv, bounds, lse, d_out)


def feed_forward(*parts):
    return pl.pallas_call(
        ffn_kernel,
        out_shape=(
            jax.ShapeDtypeStruct((TOK, D), WIDE),
            jax.ShapeDtypeStruct((4 * TOK, D), LOW),
            jax.ShapeDtypeStruct((4 * TOK, D), LOW),
            jax.ShapeDtypeStruct((4 * TOK, D), LOW),
            jax.ShapeDtypeStruct((4 * TOK, D), LOW),
            jax.ShapeDtypeStruct((4 * TOK, D), LOW),
            jax.ShapeDtypeStruct((8, D), WIDE),
        ),
        in_specs=[pl.BlockSpec(memory_space=pltpu.SMEM)] + [VMEM] * 7,
        out_specs=(VMEM, FAR, FAR, FAR, VMEM, FAR, VMEM),
        scratch_shapes=[
            pltpu.VMEM((4 * TOK, D), WIDE),
            pltpu.VMEM((D, D), LOW),
            pltpu.VMEM((D, D), LOW),
            pltpu.VMEM((4 * TOK, D), LOW),
            pltpu.VMEM((4 * TOK, D), LOW),
            pltpu.VMEM((4 * TOK, D), LOW),
            pltpu.VMEM((4 * TOK, D), LOW),
            pltpu.VMEM((4 * TOK, D), LOW),
            pltpu.SemaphoreType.DMA((4,)),
        ],
        compiler_params=WHOLE,
        cost_estimate=pl.CostEstimate(
            flops=4_000_000_000, bytes_accessed=12_000_000, transcendentals=400_000
        ),
    )(*parts)


def weight_grads(*parts):
    return pl.pallas_call(
        grad_kernel,
        out_shape=jax.ShapeDtypeStruct((8, 4 * TOK, D // 2), LOW),
        in_specs=[VMEM] * 6,
        out_specs=VMEM,
        scratch_shapes=[pltpu.VMEM((4 * TOK, D), LOW)],
        compiler_params=PARAMS,
        cost_estimate=pl.CostEstimate(
            flops=1_400_000_000, bytes_accessed=9_000_000, transcendentals=0
        ),
    )(*parts)


def tail(*parts):
    return pl.pallas_call(
        tail_kernel,
        out_shape=(
            jax.ShapeDtypeStruct((4 * TOK, D), LOW),
            jax.ShapeDtypeStruct((2, 4, 192, D // 2), LOW),
        ),
        in_specs=[pl.BlockSpec(memory_space=pltpu.SMEM)] + [VMEM] * 8,
        out_specs=(VMEM, VMEM),
        scratch_shapes=[pltpu.VMEM((4 * TOK, D), WIDE)],
        compiler_params=PARAMS,
        cost_estimate=pl.CostEstimate(
            flops=1_000_000_000, bytes_accessed=7_000_000, transcendentals=0
        ),
    )(*parts)


def pack(*parts):
    return pl.pallas_call(
        pack_kernel,
        out_shape=(
            jax.ShapeDtypeStruct((4, TOK + 96, D), LOW),
            jax.ShapeDtypeStruct((240, D), LOW),
        ),
        in_specs=[FAR] * 5 + [VMEM] * 3,
        out_specs=(VMEM, VMEM),
        scratch_shapes=[
            pltpu.VMEM((TOK, D), LOW),
            pltpu.VMEM((48, 3 * D), LOW),
            pltpu.VMEM((48, 4 * D), LOW),
            pltpu.SemaphoreType.DMA((5,)),
        ],
        compiler_params=WHOLE,
        cost_estimate=pl.CostEstimate(
            flops=1_000_000, bytes_accessed=2_500_000, transcendentals=0
        ),
    )(*parts)


def unpack(core, mine, theirs):
    return pl.pallas_call(
        unpack_kernel,
        out_shape=tuple(
            jax.ShapeDtypeStruct(shape, WIDE)
            for shape in ((48, 3 * D), (48, D), (48, 4 * D), (192, D))
            + ((1, 48),) * 3
            + ((1, 192),)
            + ((1, 48),) * 5
        ),
        in_specs=[pl.BlockSpec(memory_space=pltpu.SMEM), VMEM, VMEM],
        out_specs=(VMEM,) * 13,
        compiler_params=PARAMS,
        cost_estimate=pl.CostEstimate(
            flops=1_000_000, bytes_accessed=3_500_000, transcendentals=0
        ),
    )(core, mine, theirs)


def norm_parts(values):
    average = jnp.mean(values, axis=-1, keepdims=True)
    centered = values - average
    variance = jnp.mean(centered * centered, axis=-1, keepdims=True)
    inverse = lax.rsqrt(variance + 1e-05)
    return centered * inverse, inverse


def norm_back(hat, inverse, gain, grad):
    scaled = grad * gain
    mean_one = jnp.mean(scaled, axis=-1, keepdims=True)
    mean_two = jnp.mean(scaled * hat, axis=-1, keepdims=True)
    return inverse * (scaled - mean_one - hat * mean_two)


def swap(value, axis):
    return lax.all_to_all(value, axis, 0, 0, tiled=True)


def share(value, axis):
    return swap(jnp.broadcast_to(value[None], (4,) + value.shape), axis)


def total(value):
    return jnp.sum(value.astype(WIDE), axis=0)


def other_core(value):
    return lax.ppermute(value, "c", [(0, 1), (1, 0)])


def body(
    tokens,
    segments,
    w_qkv,
    w_out,
    w_up,
    w_down,
    b_query,
    b_value,
    b_out,
    b_up,
    b_down,
    ln1_gain,
    ln1_shift,
    ln2_gain,
    ln2_shift,
    cotangent,
):
    ix, ic, iz, iy = (lax.axis_index(name) for name in ("x", "c", "z", "y"))
    first_doc = 3 * (2 * ix + ic)
    half = D // 2

    def lanes(value, core):
        return lax.dynamic_slice_in_dim(value, core * half, half, value.ndim - 1)

    short = jnp.stack(
        [b_query, b_value, b_out, b_down, ln1_gain, ln1_shift, ln2_gain, ln2_shift]
    )
    early, plain = pack(
        tokens,
        w_qkv,
        w_up,
        w_down,
        w_out,
        short,
        b_up.reshape(4, 48),
        (segments - first_doc)[None],
    )
    early = swap(early, "z")
    token_all = early[:, :TOK].reshape(4 * TOK, D)
    seg_all = early[:, TOK + 13, 576:704].astype(jnp.int32)
    payload = early[:, TOK : TOK + 48, :640]
    payload = jnp.broadcast_to(payload[None], (4,) + payload.shape)
    early_all = swap(payload, "y").swapaxes(0, 1)
    qkv_part = early_all[:, :, :, :576].reshape(D, 3 * WIDTH)
    small_all = early_all[:, :, :16, 576:624].astype(WIDE)
    total_counts = jnp.sum(small_all[:, :, 12, :2], axis=(0, 1)).astype(jnp.int32)
    wide = small_all.reshape(16, 16, 48)[:, :8].swapaxes(0, 1).reshape(8, D)
    bias_out, bias_down, gain_one, shift_one, gain_two, shift_two = (
        wide[index] for index in range(2, 8)
    )
    own = lax.dynamic_index_in_dim(small_all, iz, 0, keepdims=False)
    bias_query = own[:, 0].reshape(WIDTH)
    bias_value = own[:, 1].reshape(WIDTH)
    bias_up = own[:, 8:12].reshape(D)

    inputs = token_all.astype(WIDE)
    hat_one, inverse_one = norm_parts(inputs)

    plain = lax.all_gather(plain, "y")
    plain, _ = lax.optimization_barrier((plain, inverse_one))
    gathered = lax.all_gather(
        jnp.concatenate([cotangent, plain[:, 192:].reshape(192, D)], axis=0), "z"
    )
    up_rows, gathered = lax.optimization_barrier((early[:, TOK + 48 :], gathered))
    up_part = lax.all_gather(up_rows.reshape(192, D), "y")
    out_rows = lax.dynamic_index_in_dim(gathered, iz, 0, keepdims=False)[TOK:]
    cot_all = gathered[:, :TOK].reshape(4 * TOK, D)

    start = jnp.where(
        seg_all <= 0, 0, jnp.where(seg_all <= 1, total_counts[0], total_counts[1])
    )
    place = (
        4 * TOK * jnp.arange(4, dtype=jnp.int32)[:, None]
        + TOK * iy
        + jnp.arange(TOK, dtype=jnp.int32)[None, :]
    )
    bounds = jnp.concatenate(
        [start.reshape(1, 4 * TOK), place.reshape(1, 4 * TOK), jnp.zeros((6, 4 * TOK), jnp.int32)]
    )

    normed_one = (hat_one * gain_one + shift_one).astype(LOW)
    qkv = dot(normed_one, qkv_part)
    query = ((qkv[:, :WIDTH] + bias_query).astype(LOW) * (HD**-0.5)).astype(LOW)
    kv = jnp.concatenate(
        [qkv[:, WIDTH : 2 * WIDTH], qkv[:, 2 * WIDTH :] + bias_value], axis=1
    ).astype(LOW)
    kv_all = share(kv, "y")
    att_part, lse = attend_forward(query, kv_all, bounds)
    att_all = swap(att_part, "z")

    middle, normed_two, activated, d_upward, d_normed, out_part, sums = feed_forward(
        iz.astype(jnp.int32)[None], early, att_all, gathered, up_part, plain, wide, bias_up[None]
    )
    d_normed = total(swap(d_normed.reshape(4, TOK, D), "z"))
    own_rows = iz * TOK

    def mine(value):
        return lax.dynamic_slice_in_dim(value, own_rows, TOK, 0)

    hat_two, inverse_two = norm_parts(middle)
    d_middle = cotangent.astype(WIDE) + norm_back(hat_two, inverse_two, gain_two, d_normed)
    d_branch = d_middle.astype(LOW)
    branch_all = share(d_branch, "z").reshape(4 * TOK, D)
    d_attended = dot(branch_all, out_rows, ((1,), (1,))).astype(LOW)

    d_query, d_kv = attend_backward(query, kv_all, bounds, lse, d_attended)

    first = weight_grads(normed_two, d_upward, activated, gathered, att_part, branch_all)
    first = lax.psum_scatter(first, ("x", "c"), scatter_dimension=0, tiled=True)
    first = first.reshape(4 * TOK, half)
    first = lax.psum_scatter(first, "y", scatter_dimension=0, tiled=True)
    d_kv = swap(d_kv, "y")
    d_normed, second = tail(
        iz.astype(jnp.int32)[None],
        d_kv,
        d_query,
        qkv_part,
        normed_one,
        early,
        sums,
        d_branch,
        cotangent,
    )
    got = other_core(lax.dynamic_index_in_dim(second, 1 - ic, 0, keepdims=False))
    second = lax.dynamic_index_in_dim(second, ic, 0, keepdims=False)
    second = (second.astype(WIDE) + got.astype(WIDE)).astype(LOW)
    second, late_normed = lax.optimization_barrier((second, d_normed))
    second = total(swap(second, "y")).astype(LOW)
    last = jnp.concatenate([late_normed, out_part], axis=1).reshape(4, TOK, 2 * D)
    last = lax.psum_scatter(last, "z", scatter_dimension=0).astype(WIDE)
    d_normed = last[:, :D]
    out_tokens = (middle + last[:, D:] + bias_down).astype(LOW)
    d_tokens = (
        d_middle + norm_back(mine(hat_one), mine(inverse_one), gain_one, d_normed)
    ).astype(LOW)

    here_x = (jnp.arange(4) == ix)[:, None, None, None]
    spread = jnp.pad(second.reshape(4, 48, half), ((0, 0), (0, 16), (0, 0)))
    joint = jnp.concatenate(
        [
            jnp.where(here_x, first[:64].reshape(1, 4, 16, half), jnp.zeros((), LOW)),
            spread.reshape(4, 4, 16, half).swapaxes(0, 1),
        ],
        axis=2,
    ).reshape(16, 32, half)
    joint = total(swap(joint, ("x", "z")).reshape(4, 4, 32, half)).astype(LOW)
    rows = first[64:]
    whole = share(jnp.concatenate([joint.reshape(TOK, half), rows], axis=0), "x")
    theirs = other_core(whole)
    grads = unpack(ic.astype(jnp.int32)[None], whole, theirs)
    return (out_tokens, d_tokens) + grads[:4] + tuple(item[0] for item in grads[4:])


def solution(mesh):
    parts = Mesh(mesh.devices.reshape(4, 2, 4, 4), ("x", "c", "z", "y"))
    every = ("x", "c", "z", "y")
    group = ("z", "y")
    row, line = P(group, None), P(group)
    return jax.shard_map(
        body,
        mesh=parts,
        in_specs=(P(every, None), P(every)) + (row,) * 4 + (line,) * 9 + (P(every, None),),
        out_specs=(P(every, None),) * 2 + (row,) * 4 + (line,) * 9,
        check_vma=False,
    )
```

```python
import jax
import jax.numpy as jnp
from jax import lax
from jax.experimental import pallas as pl
from jax.experimental.pallas import tpu as pltpu
from jax.sharding import Mesh, PartitionSpec as P

HD = 64
TOK = 128
D = 768
HEADS = 3
WIDTH = HEADS * HD
CHUNK = 512
LOW = jnp.bfloat16
WIDE = jnp.float32


def dot(left, right, dims=((1,), (0,))):
    return lax.dot_general(left, right, (dims, ((), ())), preferred_element_type=WIDE)


def masked(scores, start, place, chunk, block):
    if chunk != block and chunk != 0 and block != 3:
        return scores
    spots = lax.broadcasted_iota(jnp.int32, scores.shape, 0) + chunk * CHUNK
    allowed = None
    if chunk == 0 or block == 3:
        allowed = spots >= start
    if chunk == block:
        causal = spots <= place
        allowed = causal if allowed is None else allowed & causal
    return jnp.where(allowed, scores, -1e30)


def chunk_rows(kv_ref, chunk, low, high):
    return jnp.concatenate(
        [kv_ref[y, chunk * TOK : (chunk + 1) * TOK, low:high] for y in range(4)], axis=0
    )


def forward_kernel(q_ref, kv_ref, bound_ref, att_ref, lse_ref):
    for block in range(4):
        rows = slice(block * TOK, (block + 1) * TOK)
        start = bound_ref[0:1, rows]
        place = bound_ref[1:2, rows]
        for head in range(HEADS):
            cols = slice(head * HD, (head + 1) * HD)
            query = q_ref[rows, cols]
            scores = []
            for chunk in range(block + 1):
                keys = chunk_rows(kv_ref, chunk, head * HD, head * HD + HD)
                scores.append(
                    masked(dot(keys, query, ((1,), (1,))), start, place, chunk, block)
                )
            top = scores[0].max(axis=0, keepdims=True)
            for item in scores[1:]:
                top = jnp.maximum(top, item.max(axis=0, keepdims=True))
            total = jnp.zeros((1, TOK), WIDE)
            summed = jnp.zeros((HD, TOK), WIDE)
            for chunk in range(block + 1):
                weights = jnp.exp(scores[chunk] - top)
                total = total + weights.sum(axis=0, keepdims=True)
                values = chunk_rows(kv_ref, chunk, WIDTH + head * HD, WIDTH + head * HD + HD)
                summed = summed + dot(values, weights.astype(LOW), ((0,), (0,)))
            att_ref[rows, cols] = jnp.transpose(summed / total).astype(LOW)
            lse_ref[head : head + 1, rows] = top + jnp.log(total)


def backward_kernel(q_ref, kv_ref, bound_ref, lse_ref, do_ref, dq_ref, dkv_ref, p_ref, ds_ref):
    for head in range(HEADS):
        cols = slice(head * HD, (head + 1) * HD)
        for block in range(4):
            rows = slice(block * TOK, (block + 1) * TOK)
            start = bound_ref[0:1, rows]
            place = bound_ref[1:2, rows]
            query = q_ref[rows, cols]
            d_out = do_ref[rows, cols]
            lse = lse_ref[head : head + 1, rows]
            delta = jnp.zeros((1, TOK), WIDE)
            probs, d_probs = [], []
            for chunk in range(block + 1):
                keys = chunk_rows(kv_ref, chunk, head * HD, head * HD + HD)
                scores = masked(dot(keys, query, ((1,), (1,))), start, place, chunk, block)
                prob = jnp.exp(scores - lse)
                values = chunk_rows(kv_ref, chunk, WIDTH + head * HD, WIDTH + head * HD + HD)
                d_prob = dot(values, d_out, ((1,), (1,)))
                delta = delta + (prob * d_prob).sum(axis=0, keepdims=True)
                p_ref[chunk * CHUNK : (chunk + 1) * CHUNK, rows] = prob.astype(LOW)
                probs.append(prob)
                d_probs.append(d_prob)
            d_query = jnp.zeros((HD, TOK), WIDE)
            for chunk in range(block + 1):
                d_score = (probs[chunk] * (d_probs[chunk] - delta)).astype(LOW)
                ds_ref[chunk * CHUNK : (chunk + 1) * CHUNK, rows] = d_score
                keys = chunk_rows(kv_ref, chunk, head * HD, head * HD + HD)
                d_query = d_query + dot(keys, d_score, ((0,), (0,)))
            dq_ref[rows, cols] = (jnp.transpose(d_query) * (HD**-0.5)).astype(LOW)
        for chunk in range(4):
            spots = slice(chunk * CHUNK, (chunk + 1) * CHUNK)
            later = slice(chunk * TOK, 4 * TOK)
            d_keys = dot(ds_ref[spots, later], q_ref[later, cols]).astype(LOW)
            d_values = dot(p_ref[spots, later], do_ref[later, cols]).astype(LOW)
            for y in range(4):
                part = slice(y * TOK, (y + 1) * TOK)
                place_rows = slice(chunk * TOK, (chunk + 1) * TOK)
                dkv_ref[y, place_rows, cols] = d_keys[part]
                dkv_ref[y, place_rows, WIDTH + head * HD : WIDTH + head * HD + HD] = d_values[part]


def ffn_kernel(
    own_ref,
    early_ref,
    att_ref,
    gathered_ref,
    up_ref,
    plain_ref,
    wide_ref,
    bias_ref,
    middle_ref,
    normed_hbm,
    act_hbm,
    d_up_hbm,
    d_normed_ref,
    out_hbm,
    sums_ref,
    mid_scr,
    up_scr,
    down_scr,
    cot_scr,
    normed_ref,
    act_ref,
    d_up_ref,
    out_ref,
    sems,
):
    copies = [
        pltpu.make_async_copy(source, target, sems.at[index])
        for index, (source, target) in enumerate(
            (
                (normed_ref, normed_hbm),
                (act_ref, act_hbm),
                (d_up_ref, d_up_hbm),
                (out_ref, out_hbm),
            )
        )
    ]
    for z in range(4):
        for y in range(4):
            row = (4 * z + y) * 48
            up_scr[row : row + 48] = up_ref[y, 48 * z : 48 * z + 48]
        down_scr[192 * z : 192 * z + 192] = plain_ref[z, 0:192]
        cot_scr[TOK * z : TOK * z + TOK] = gathered_ref[z, 0:TOK]
        mid_scr[TOK * z : TOK * z + TOK] = early_ref[z, 0:TOK].astype(WIDE)
    middle = mid_scr[...] + wide_ref[2:3, :]
    for z in range(4):
        middle = middle + dot(att_ref[z], gathered_ref[z, TOK : TOK + 192])
    mid_scr[...] = middle
    middle_ref[...] = mid_scr[pl.ds(pl.multiple_of(own_ref[0] * TOK, TOK), TOK), :]
    average = jnp.mean(middle, axis=-1, keepdims=True)
    centered = middle - average
    variance = jnp.mean(centered * centered, axis=-1, keepdims=True)
    hat = centered * lax.rsqrt(variance + 1e-05)
    normed = (hat * wide_ref[6:7, :] + wide_ref[7:8, :]).astype(LOW)
    normed_ref[...] = normed
    copies[0].start()
    upward = dot(normed, up_scr[...]) + bias_ref[...]
    root = 0.7978845608028654
    square = upward * upward
    bend = jnp.tanh(root * (upward + 0.044715 * (square * upward)))
    level = 0.5 * (1.0 + bend)
    activated = (upward * level).astype(LOW)
    act_ref[...] = activated
    copies[1].start()
    out_ref[...] = dot(activated, down_scr[...]).astype(LOW)
    copies[3].start()
    slope = level + 0.5 * upward * (1.0 - bend * bend) * (root * (1.0 + 0.134145 * square))
    d_act = dot(cot_scr[...], down_scr[...], ((1,), (1,)))
    d_upward = (d_act * slope).astype(LOW)
    d_up_ref[...] = d_upward
    copies[2].start()
    d_normed = dot(d_upward, up_scr[...], ((1,), (1,)))
    d_normed_ref[...] = d_normed.astype(LOW)
    sums_ref[0:1, :] = jnp.sum(d_normed * hat, axis=0, keepdims=True)
    sums_ref[1:2, :] = jnp.sum(d_normed, axis=0, keepdims=True)
    sums_ref[2:3, :] = jnp.sum(d_upward.astype(WIDE), axis=0, keepdims=True)
    sums_ref[3:8, :] = jnp.zeros((5, D), WIDE)
    for copy in copies:
        copy.wait()


def grad_kernel(normed_ref, d_up_ref, act_ref, gathered_ref, att_ref, branch_ref, out_ref, cot_scr):
    half = D // 2
    for z in range(4):
        cot_scr[TOK * z : TOK * z + TOK] = gathered_ref[z, 0:TOK]
    up = dot(normed_ref[...], d_up_ref[...], ((0,), (0,))).astype(LOW)
    down = dot(act_ref[...], cot_scr[...], ((0,), (0,))).astype(LOW)
    proj = dot(att_ref[...], branch_ref[...], ((0,), (0,))).astype(LOW)
    blank = jnp.zeros((16, half), LOW)
    for x in range(4):
        for core in range(2):
            cols = slice(core * half, core * half + half)
            slot = 2 * x + core
            for y in range(4):
                base = TOK * y
                for z in range(4):
                    row = (4 * z + y) * 48 + 16 * x
                    out_ref[slot, base + 16 * z : base + 16 * z + 16] = (
                        up[row : row + 16, cols] if x < 3 else blank
                    )
                row = 192 * y + 48 * x
                out_ref[slot, base + 64 : base + 112] = down[row : row + 48, cols]
                row = 48 * y + 16 * x
                out_ref[slot, base + 112 : base + 128] = (
                    proj[row : row + 16, cols] if x < 3 else blank
                )


def tail_kernel(
    own_ref,
    moved_ref,
    query_ref,
    weight_ref,
    normed_ref,
    early_ref,
    sums_ref,
    branch_ref,
    cot_ref,
    d_normed_ref,
    out_ref,
    hat_scr,
):
    half = D // 2
    for z in range(4):
        hat_scr[TOK * z : TOK * z + TOK] = early_ref[z, 0:TOK].astype(WIDE)
    inputs = hat_scr[...]
    centered = inputs - jnp.mean(inputs, axis=-1, keepdims=True)
    variance = jnp.mean(centered * centered, axis=-1, keepdims=True)
    hat = centered * lax.rsqrt(variance + 1e-05)
    d_kv = moved_ref[0].astype(WIDE)
    for y in range(1, 4):
        d_kv = d_kv + moved_ref[y].astype(WIDE)
    d_qkv = jnp.concatenate([query_ref[...].astype(WIDE), d_kv], axis=1).astype(LOW)
    d_normed = dot(d_qkv, weight_ref[...], ((1,), (1,)))
    d_normed_ref[...] = d_normed.astype(LOW)
    d_weight = dot(normed_ref[...], d_qkv, ((0,), (0,)))
    columns = jnp.sum(d_qkv.astype(WIDE), axis=0, keepdims=True)
    wide_rows = [
        jnp.sum(branch_ref[...].astype(WIDE), axis=0, keepdims=True),
        jnp.sum(cot_ref[...].astype(WIDE), axis=0, keepdims=True),
        jnp.sum(d_normed * hat, axis=0, keepdims=True),
        jnp.sum(d_normed, axis=0, keepdims=True),
        sums_ref[0:1, :],
        sums_ref[1:2, :],
    ]
    hidden = sums_ref[2:3, :]
    for y in range(4):
        low = 48 * y
        own_rows = [
            columns[:, low : low + 48],
            columns[:, 2 * WIDTH + low : 2 * WIDTH + low + 48],
        ] + [hidden[:, 192 * y + 48 * i : 192 * y + 48 * i + 48] for i in range(4)]
        own_rows = jnp.concatenate(own_rows, axis=0)
        for z in range(4):
            low = 48 * (4 * z + y)
            short = jnp.concatenate(
                [jnp.where(own_ref[0] == z, own_rows, 0.0)]
                + [item[:, low : low + 48] for item in wide_rows]
                + [jnp.zeros((36, 48), WIDE)],
                axis=0,
            )
            block = d_weight[low : low + 48]
            out_ref[0, y, 48 * z : 48 * z + 48] = block[:, :half].astype(LOW)
            out_ref[1, y, 48 * z : 48 * z + 48] = jnp.concatenate(
                [block[:, half:], short, jnp.zeros((48, 144), WIDE)], axis=1
            ).astype(LOW)


def pack_kernel(
    tokens_hbm,
    qkv_hbm,
    up_hbm,
    down_hbm,
    proj_hbm,
    short_ref,
    hidden_ref,
    seg_ref,
    out_ref,
    plain_ref,
    tokens_ref,
    qkv_ref,
    up_ref,
    sems,
):
    pairs = (
        (tokens_hbm, tokens_ref),
        (qkv_hbm, qkv_ref),
        (up_hbm, up_ref),
        (down_hbm, plain_ref.at[pl.ds(0, 192)]),
        (proj_hbm, plain_ref.at[pl.ds(192, 48)]),
    )
    copies = [
        pltpu.make_async_copy(source, target, sems.at[index])
        for index, (source, target) in enumerate(pairs)
    ]
    for copy in copies:
        copy.start()
    seg = seg_ref[...]
    count_one = jnp.sum((seg <= 0).astype(WIDE), axis=1, keepdims=True)
    count_two = jnp.sum((seg <= 1).astype(WIDE), axis=1, keepdims=True)
    spot = lax.broadcasted_iota(jnp.int32, (1, 192), 1)
    counts = jnp.where(spot == 0, count_one, jnp.where(spot == 1, count_two, 0.0))
    side = jnp.concatenate(
        [
            jnp.concatenate(
                [short_ref[...].astype(WIDE), jnp.zeros((8, 144), WIDE)], axis=1
            ),
            jnp.concatenate(
                [hidden_ref[...].astype(WIDE), jnp.zeros((4, 144), WIDE)], axis=1
            ),
            counts,
            jnp.concatenate([seg.astype(WIDE), jnp.zeros((1, 64), WIDE)], axis=1),
            jnp.zeros((34, 192), WIDE),
        ],
        axis=0,
    ).astype(LOW)
    for copy in copies:
        copy.wait()
    for part in range(4):
        out_ref[part, 0:TOK, :] = tokens_ref[...]
        for kind in range(3):
            out_ref[part, TOK : TOK + 48, kind * WIDTH : (kind + 1) * WIDTH] = qkv_ref[
                :, kind * D + part * WIDTH : kind * D + (part + 1) * WIDTH
            ]
        out_ref[part, TOK : TOK + 48, 3 * WIDTH : D] = side
        out_ref[part, TOK + 48 : TOK + 96, :] = up_ref[:, part * D : (part + 1) * D]


def unpack_kernel(core_ref, mine_ref, theirs_ref, qkv_ref, out_ref, up_ref, down_ref, *line_refs):
    first = core_ref[0] == 0
    half = D // 2
    short = jnp.zeros((12, 48), WIDE)
    for part in range(4):
        mine = mine_ref[part].astype(WIDE)
        theirs = theirs_ref[part].astype(WIDE)
        sides = (jnp.where(first, mine, theirs), jnp.where(first, theirs, mine))
        rows = slice(16 * part, 16 * part + 16)
        for core in range(2):
            side = sides[core]
            cols = slice(core * half, (core + 1) * half)
            down_ref[part * 48 : (part + 1) * 48, cols] = side[TOK : TOK + 48]
            if part == 3:
                continue
            out_ref[rows, cols] = side[TOK + 48 : TOK + 64]
            for quarter in range(4):
                low = quarter * D + core * half
                up_ref[rows, low : low + half] = side[32 * quarter : 32 * quarter + 16]
                block = side[32 * quarter + 16 : 32 * quarter + 32]
                low = quarter * WIDTH
                if core == 0:
                    qkv_ref[rows, low : low + WIDTH] = block[:, :WIDTH]
                    qkv_ref[rows, D + low : D + low + WIDTH] = block[:, WIDTH:]
                else:
                    qkv_ref[rows, 2 * D + low : 2 * D + low + WIDTH] = block[:, :WIDTH]
                    if part == 0:
                        short = short + block[:12, WIDTH : WIDTH + 48]
    hidden = jnp.concatenate([short[2 + i : 3 + i] for i in range(4)], axis=1)
    lines = [short[i : i + 1] for i in (0, 1, 6)] + [hidden]
    lines += [short[i : i + 1] for i in range(7, 12)]
    for ref, value in zip(line_refs, lines):
        ref[...] = value


VMEM = pl.BlockSpec(memory_space=pltpu.VMEM)
FAR = pl.BlockSpec(memory_space=pltpu.HBM)
PARAMS = pltpu.CompilerParams(vmem_limit_bytes=48 * 1024 * 1024)
WHOLE = pltpu.CompilerParams(vmem_limit_bytes=60 * 1024 * 1024)


def attend_forward(query, kv, bounds):
    return pl.pallas_call(
        forward_kernel,
        out_shape=(
            jax.ShapeDtypeStruct((4 * TOK, WIDTH), LOW),
            jax.ShapeDtypeStruct((8, 4 * TOK), WIDE),
        ),
        in_specs=[VMEM] * 3,
        out_specs=(VMEM, VMEM),
        compiler_params=PARAMS,
        cost_estimate=pl.CostEstimate(
            flops=1_000_000_000, bytes_accessed=4_000_000, transcendentals=2_000_000
        ),
    )(query, kv, bounds)


def attend_backward(query, kv, bounds, lse, d_out):
    return pl.pallas_call(
        backward_kernel,
        out_shape=(
            jax.ShapeDtypeStruct((4 * TOK, WIDTH), LOW),
            jax.ShapeDtypeStruct((4, 4 * TOK, 2 * WIDTH), LOW),
        ),
        in_specs=[VMEM] * 5,
        out_specs=(VMEM, VMEM),
        scratch_shapes=[
            pltpu.VMEM((4 * CHUNK, 4 * TOK), LOW),
            pltpu.VMEM((4 * CHUNK, 4 * TOK), LOW),
        ],
        compiler_params=WHOLE,
        cost_estimate=pl.CostEstimate(
            flops=2_500_000_000, bytes_accessed=6_000_000, transcendentals=2_000_000
        ),
    )(query, kv, bounds, lse, d_out)


def feed_forward(*parts):
    return pl.pallas_call(
        ffn_kernel,
        out_shape=(
            jax.ShapeDtypeStruct((TOK, D), WIDE),
            jax.ShapeDtypeStruct((4 * TOK, D), LOW),
            jax.ShapeDtypeStruct((4 * TOK, D), LOW),
            jax.ShapeDtypeStruct((4 * TOK, D), LOW),
            jax.ShapeDtypeStruct((4 * TOK, D), LOW),
            jax.ShapeDtypeStruct((4 * TOK, D), LOW),
            jax.ShapeDtypeStruct((8, D), WIDE),
        ),
        in_specs=[pl.BlockSpec(memory_space=pltpu.SMEM)] + [VMEM] * 7,
        out_specs=(VMEM, FAR, FAR, FAR, VMEM, FAR, VMEM),
        scratch_shapes=[
            pltpu.VMEM((4 * TOK, D), WIDE),
            pltpu.VMEM((D, D), LOW),
            pltpu.VMEM((D, D), LOW),
            pltpu.VMEM((4 * TOK, D), LOW),
            pltpu.VMEM((4 * TOK, D), LOW),
            pltpu.VMEM((4 * TOK, D), LOW),
            pltpu.VMEM((4 * TOK, D), LOW),
            pltpu.VMEM((4 * TOK, D), LOW),
            pltpu.SemaphoreType.DMA((4,)),
        ],
        compiler_params=WHOLE,
        cost_estimate=pl.CostEstimate(
            flops=4_000_000_000, bytes_accessed=12_000_000, transcendentals=400_000
        ),
    )(*parts)


def weight_grads(*parts):
    return pl.pallas_call(
        grad_kernel,
        out_shape=jax.ShapeDtypeStruct((8, 4 * TOK, D // 2), LOW),
        in_specs=[VMEM] * 6,
        out_specs=VMEM,
        scratch_shapes=[pltpu.VMEM((4 * TOK, D), LOW)],
        compiler_params=WHOLE,
        cost_estimate=pl.CostEstimate(
            flops=1_400_000_000, bytes_accessed=9_000_000, transcendentals=0
        ),
    )(*parts)


def tail(*parts):
    return pl.pallas_call(
        tail_kernel,
        out_shape=(
            jax.ShapeDtypeStruct((4 * TOK, D), LOW),
            jax.ShapeDtypeStruct((2, 4, 192, D // 2), LOW),
        ),
        in_specs=[pl.BlockSpec(memory_space=pltpu.SMEM)] + [VMEM] * 8,
        out_specs=(VMEM, VMEM),
        scratch_shapes=[pltpu.VMEM((4 * TOK, D), WIDE)],
        compiler_params=WHOLE,
        cost_estimate=pl.CostEstimate(
            flops=1_000_000_000, bytes_accessed=7_000_000, transcendentals=0
        ),
    )(*parts)


def pack(*parts):
    return pl.pallas_call(
        pack_kernel,
        out_shape=(
            jax.ShapeDtypeStruct((4, TOK + 96, D), LOW),
            jax.ShapeDtypeStruct((240, D), LOW),
        ),
        in_specs=[FAR] * 5 + [VMEM] * 3,
        out_specs=(VMEM, VMEM),
        scratch_shapes=[
            pltpu.VMEM((TOK, D), LOW),
            pltpu.VMEM((48, 3 * D), LOW),
            pltpu.VMEM((48, 4 * D), LOW),
            pltpu.SemaphoreType.DMA((5,)),
        ],
        compiler_params=WHOLE,
        cost_estimate=pl.CostEstimate(
            flops=1_000_000, bytes_accessed=2_500_000, transcendentals=0
        ),
    )(*parts)


def unpack(core, mine, theirs):
    return pl.pallas_call(
        unpack_kernel,
        out_shape=tuple(
            jax.ShapeDtypeStruct(shape, WIDE)
            for shape in ((48, 3 * D), (48, D), (48, 4 * D), (192, D))
            + ((1, 48),) * 3
            + ((1, 192),)
            + ((1, 48),) * 5
        ),
        in_specs=[pl.BlockSpec(memory_space=pltpu.SMEM), VMEM, VMEM],
        out_specs=(VMEM,) * 13,
        compiler_params=PARAMS,
        cost_estimate=pl.CostEstimate(
            flops=1_000_000, bytes_accessed=3_500_000, transcendentals=0
        ),
    )(core, mine, theirs)


def norm_parts(values):
    average = jnp.mean(values, axis=-1, keepdims=True)
    centered = values - average
    variance = jnp.mean(centered * centered, axis=-1, keepdims=True)
    inverse = lax.rsqrt(variance + 1e-05)
    return centered * inverse, inverse


def norm_back(hat, inverse, gain, grad):
    scaled = grad * gain
    mean_one = jnp.mean(scaled, axis=-1, keepdims=True)
    mean_two = jnp.mean(scaled * hat, axis=-1, keepdims=True)
    return inverse * (scaled - mean_one - hat * mean_two)


def swap(value, axis):
    return lax.all_to_all(value, axis, 0, 0, tiled=True)


def share(value, axis):
    return swap(jnp.broadcast_to(value[None], (4,) + value.shape), axis)


def total(value):
    return jnp.sum(value.astype(WIDE), axis=0)


def other_core(value):
    return lax.ppermute(value, "c", [(0, 1), (1, 0)])


def body(
    tokens,
    segments,
    w_qkv,
    w_out,
    w_up,
    w_down,
    b_query,
    b_value,
    b_out,
    b_up,
    b_down,
    ln1_gain,
    ln1_shift,
    ln2_gain,
    ln2_shift,
    cotangent,
):
    ix, ic, iz, iy = (lax.axis_index(name) for name in ("x", "c", "z", "y"))
    first_doc = 3 * (2 * ix + ic)
    half = D // 2

    def lanes(value, core):
        return lax.dynamic_slice_in_dim(value, core * half, half, value.ndim - 1)

    short = jnp.stack(
        [b_query, b_value, b_out, b_down, ln1_gain, ln1_shift, ln2_gain, ln2_shift]
    )
    early, plain = pack(
        tokens,
        w_qkv,
        w_up,
        w_down,
        w_out,
        short,
        b_up.reshape(4, 48),
        (segments - first_doc)[None],
    )
    early = swap(early, "z")
    token_all = early[:, :TOK].reshape(4 * TOK, D)
    seg_all = early[:, TOK + 13, 576:704].astype(jnp.int32)
    payload = early[:, TOK : TOK + 48, :640]
    payload = jnp.broadcast_to(payload[None], (4,) + payload.shape)
    early_all = swap(payload, "y").swapaxes(0, 1)
    qkv_part = early_all[:, :, :, :576].reshape(D, 3 * WIDTH)
    small_all = early_all[:, :, :16, 576:624].astype(WIDE)
    total_counts = jnp.sum(small_all[:, :, 12, :2], axis=(0, 1)).astype(jnp.int32)
    wide = small_all.reshape(16, 16, 48)[:, :8].swapaxes(0, 1).reshape(8, D)
    bias_out, bias_down, gain_one, shift_one, gain_two, shift_two = (
        wide[index] for index in range(2, 8)
    )
    own = lax.dynamic_index_in_dim(small_all, iz, 0, keepdims=False)
    bias_query = own[:, 0].reshape(WIDTH)
    bias_value = own[:, 1].reshape(WIDTH)
    bias_up = own[:, 8:12].reshape(D)

    plain = lax.all_gather(plain, "y")
    plain, _ = lax.optimization_barrier((plain, payload))
    gathered = lax.all_gather(
        jnp.concatenate([cotangent, plain[:, 192:].reshape(192, D)], axis=0), "z"
    )
    up_rows, gathered = lax.optimization_barrier((early[:, TOK + 48 :], gathered))
    up_part = lax.all_gather(up_rows.reshape(192, D), "y")
    out_rows = lax.dynamic_index_in_dim(gathered, iz, 0, keepdims=False)[TOK:]
    cot_all = gathered[:, :TOK].reshape(4 * TOK, D)

    inputs = token_all.astype(WIDE)
    start = jnp.where(
        seg_all <= 0, 0, jnp.where(seg_all <= 1, total_counts[0], total_counts[1])
    )
    place = (
        4 * TOK * jnp.arange(4, dtype=jnp.int32)[:, None]
        + TOK * iy
        + jnp.arange(TOK, dtype=jnp.int32)[None, :]
    )
    bounds = jnp.concatenate(
        [start.reshape(1, 4 * TOK), place.reshape(1, 4 * TOK), jnp.zeros((6, 4 * TOK), jnp.int32)]
    )

    hat_one, inverse_one = norm_parts(inputs)
    normed_one = (hat_one * gain_one + shift_one).astype(LOW)
    qkv = dot(normed_one, qkv_part)
    query = ((qkv[:, :WIDTH] + bias_query).astype(LOW) * (HD**-0.5)).astype(LOW)
    kv = jnp.concatenate(
        [qkv[:, WIDTH : 2 * WIDTH], qkv[:, 2 * WIDTH :] + bias_value], axis=1
    ).astype(LOW)
    kv_all = share(kv, "y")
    att_part, lse = attend_forward(query, kv_all, bounds)
    att_all = share(att_part, "z")

    middle, normed_two, activated, d_upward, d_normed, out_part, sums = feed_forward(
        iz.astype(jnp.int32)[None], early, att_all, gathered, up_part, plain, wide, bias_up[None]
    )
    d_normed = total(swap(d_normed.reshape(4, TOK, D), "z"))
    own_rows = iz * TOK

    def mine(value):
        return lax.dynamic_slice_in_dim(value, own_rows, TOK, 0)

    hat_two, inverse_two = norm_parts(middle)
    d_middle = cotangent.astype(WIDE) + norm_back(hat_two, inverse_two, gain_two, d_normed)
    d_branch = d_middle.astype(LOW)
    branch_all = share(d_branch, "z").reshape(4 * TOK, D)
    d_attended = dot(branch_all, out_rows, ((1,), (1,))).astype(LOW)

    d_query, d_kv = attend_backward(query, kv_all, bounds, lse, d_attended)

    first = weight_grads(normed_two, d_upward, activated, gathered, att_part, branch_all)
    first = lax.psum_scatter(first, ("x", "c"), scatter_dimension=0, tiled=True)
    d_kv = swap(d_kv, "y")
    d_normed, second = tail(
        iz.astype(jnp.int32)[None],
        d_kv,
        d_query,
        qkv_part,
        normed_one,
        early,
        sums,
        d_branch,
        cotangent,
    )
    got = other_core(lax.dynamic_index_in_dim(second, 1 - ic, 0, keepdims=False))
    second = lax.dynamic_index_in_dim(second, ic, 0, keepdims=False)
    second = (second.astype(WIDE) + got.astype(WIDE)).astype(LOW)
    second, late_normed = lax.optimization_barrier((second, d_normed))
    second = jnp.concatenate([first.reshape(4, TOK, half), second], axis=1)
    second = total(swap(second, "y")).astype(LOW)
    last = jnp.concatenate([late_normed, out_part], axis=1).reshape(4, TOK, 2 * D)
    last = lax.psum_scatter(last, "z", scatter_dimension=0).astype(WIDE)
    d_normed = last[:, :D]
    out_tokens = (middle + last[:, D:] + bias_down).astype(LOW)
    d_tokens = (
        d_middle + norm_back(mine(hat_one), mine(inverse_one), gain_one, d_normed)
    ).astype(LOW)

    here_x = (jnp.arange(4) == ix)[:, None, None, None]
    spread = jnp.pad(second[TOK:].reshape(4, 48, half), ((0, 0), (0, 16), (0, 0)))
    joint = jnp.concatenate(
        [
            jnp.where(here_x, second[:64].reshape(1, 4, 16, half), jnp.zeros((), LOW)),
            spread.reshape(4, 4, 16, half).swapaxes(0, 1),
        ],
        axis=2,
    ).reshape(16, 32, half)
    joint = total(swap(joint, ("x", "z")).reshape(4, 4, 32, half)).astype(LOW)
    rows = second[64:TOK]
    whole = share(jnp.concatenate([joint.reshape(TOK, half), rows], axis=0), "x")
    theirs = other_core(whole)
    grads = unpack(ic.astype(jnp.int32)[None], whole, theirs)
    return (out_tokens, d_tokens) + grads[:4] + tuple(item[0] for item in grads[4:])


def solution(mesh):
    parts = Mesh(mesh.devices.reshape(4, 2, 4, 4), ("x", "c", "z", "y"))
    every = ("x", "c", "z", "y")
    group = ("z", "y")
    row, line = P(group, None), P(group)
    return jax.shard_map(
        body,
        mesh=parts,
        in_specs=(P(every, None), P(every)) + (row,) * 4 + (line,) * 9 + (P(every, None),),
        out_specs=(P(every, None),) * 2 + (row,) * 4 + (line,) * 9,
        check_vma=False,
    )
```
